512 devices in a mesh: row: 8 (over y, x_hi), col: 16 (over z), occ: 4 (over x_lo, core).
Axes of the slice: x: 4 (x_hi: 2, x_lo: 2; x = x_hi * 2 + x_lo), y: 4, z: 16, core: 2. Of those that a mesh axis runs over, the one named last changes fastest.
Arguments:
- amplitudes: float32 [512, 3, 512], P(('row', 'col'), None, 'occ'), may hold values from -24 to 24
- integrals: float32 [3, 512, 512, 512], P(None, 'occ', ('row', 'col')), may hold values from -0.4375 to 0.4375
- orbital_irrep: int32 [512], replicated, may hold values from 0 to 7
- slab_irrep: int32 [3], replicated, may hold values from 0 to 7
- pair_irrep: int32 [512], replicated, may hold values from 0 to 7
Outputs:
- residual: float32 [512, 512, 512], P('occ', ('row', 'col'))
The draws below stay inside these ranges and needn't reach their ends.
Inputs may be any that keep to these rules, and one draw needn't show every extreme that they name: `orbital_irrep`: labels of the 8 irreps. `slab_irrep`: labels of the 8 irreps. `pair_irrep`: labels of the 8 irreps.
All inputs are finite; a program needn't handle non-finite values.
Results may differ from the reference program's by a relative error of at most 0.00007.
Values sent between devices are 32-bit elements; how exact they have to be, the bound alone decides.
No kernel may reach another device: no remote copies, remote signals or barrier semaphores. Data moves between devices by JAX's collectives and lax.ppermute only.
A program may use at most 128 MiB of HBM per device.

```python
import jax
import jax.numpy as jnp
from jax import lax

VIRT = 512
SLAB = 3
PAIRS = 512
IRREPS = 8


def set_ends(drawn, own_key, smallest, top_value):
    longest = drawn.shape.index(max(drawn.shape))
    spots = []
    for shift in (0, 1):
        where = [jax.random.randint(jax.random.fold_in(own_key, axis), (), 0, length) for axis, length in enumerate(drawn.shape)]
        where[longest] = (where[longest] + shift) % drawn.shape[longest]
        spots.append(tuple(where))
    return drawn.at[spots[0]].set(smallest).at[spots[1]].set(top_value)


def strengthened(array, key, source, target, blocks, factor):
    def block_of(dim):
        return (jnp.arange(array.shape[dim]) // (array.shape[dim] // blocks)).reshape((-1,) + (1,) * (array.ndim - 1 - dim))

    one_side = jax.random.permutation(key, blocks)[block_of(target)]
    other_side = (block_of(target) + blocks // 2) % blocks
    return jnp.where((block_of(source) == one_side) | (block_of(source) == other_side), factor * array, array)


def level_of(own_key, shape, cuts, smallest, high):
    level = 1.0
    for dim, shards_of in cuts:
        steps = jax.random.uniform(jax.random.fold_in(jax.random.fold_in(own_key, 6), dim), (shards_of,), jnp.float32, smallest / len(cuts), high / len(cuts))
        level = level * jnp.repeat(jnp.exp(steps), shape[dim] // shards_of).reshape((-1,) + (1,) * (len(shape) - 1 - dim))
    return level


def centred(stream_key, shape, scale, most, cuts=(), dtype=jnp.bfloat16):
    factor_of = level_of(stream_key, shape, cuts, -0.22, 0.18) if cuts else 1.0
    drawn = jax.random.normal(stream_key, shape, jnp.float32) * scale * factor_of
    return jnp.minimum(jnp.maximum(drawn, -most), most).astype(dtype)


def heavy_noise(rng, extent, scale, limit, shards, heavy, held_as=jnp.bfloat16):
    drawn = scale * jax.random.normal(rng, extent, jnp.float32)
    if shards:
        drawn = drawn * level_of(rng, extent, shards, -0.22, 0.18)
    return jnp.clip(strengthened(drawn, jax.random.fold_in(rng, 3), *heavy), -limit, limit).astype(held_as)


def setup_inputs(seed: int = 0) -> dict:
    arg_keys = jax.random.split(jax.random.key(seed), 6)
    return {
        "amplitudes": heavy_noise(arg_keys[0], (PAIRS, SLAB, VIRT), 1.0, 24.0, ((0, 128), (2, 4)), (2, 0, 128, 5.5), jnp.float32),
        "integrals": centred(arg_keys[1], (SLAB, VIRT, VIRT, VIRT), (SLAB * VIRT // 8) ** -0.5, 0.4375, ((1, 4), (2, 128)), jnp.float32),
        "orbital_irrep": set_ends(jax.random.randint(arg_keys[2], (VIRT,), 0, IRREPS), jax.random.fold_in(arg_keys[2], 1), 0, IRREPS - 1).astype(jnp.int32),
        "slab_irrep": jax.random.randint(arg_keys[3], (SLAB,), 0, IRREPS).astype(jnp.int32),
        "pair_irrep": set_ends(jax.random.randint(arg_keys[4], (PAIRS,), 0, IRREPS), jax.random.fold_in(arg_keys[4], 1), 0, IRREPS - 1).astype(jnp.int32),
    }


def reference(amplitudes, integrals, orbital_irrep, slab_irrep, pair_irrep):
    allowed = jnp.bitwise_xor(slab_irrep[:, None], orbital_irrep[None, :])
    kept_cells = allowed[None, :, :] == pair_irrep[:, None, None]
    masked = jnp.where(kept_cells, amplitudes, jnp.zeros_like(amplitudes))
    flat_ladder = jnp.dot(masked.reshape(PAIRS, SLAB * VIRT), integrals.reshape(SLAB * VIRT, VIRT * VIRT), precision=lax.Precision.HIGHEST, preferred_element_type=jnp.float32)
    ladder = flat_ladder.reshape(PAIRS, VIRT, VIRT)
    pair_label = jnp.bitwise_xor(orbital_irrep[:, None], orbital_irrep[None, :])
    ladder = jnp.where(pair_label[None, :, :] == pair_irrep[:, None, None], ladder, jnp.zeros_like(ladder))
    return ladder - jnp.transpose(ladder, (0, 2, 1))
```

```python
import functools

import jax
import jax.numpy as jnp
import numpy as np
from jax import lax
from jax.experimental import pallas as pl
from jax.experimental.pallas import tpu as pltpu
from jax.sharding import Mesh
from jax.sharding import PartitionSpec as P

SLOTS = 32
LANES = 128
VMEM = pl.BlockSpec(memory_space=pltpu.VMEM)
SMEM = pl.BlockSpec(memory_space=pltpu.SMEM)


def split(x):
    high = x.astype(jnp.bfloat16)
    return high, (x - high.astype(jnp.float32)).astype(jnp.bfloat16)


def dot(x, y):
    return jnp.dot(x, y, preferred_element_type=jnp.float32)


def column_of(row):
    return jnp.transpose(jnp.broadcast_to(row, (LANES, LANES)))


def ladder_kernel(place, slab, orbital_s, orbital, pair, gathered, integrals, keep, send, high_t, low_t):
    block, occ, core, shift = place[0], place[1], place[2], place[3]
    depth_row = orbital[pl.ds(occ, 1), :]
    depth_rows = [depth_row ^ slab[c] for c in range(3)]
    before = lax.broadcasted_iota(jnp.int32, (LANES, LANES), 0) < lax.broadcasted_iota(jnp.int32, (LANES, LANES), 1)
    slot = lax.broadcasted_iota(jnp.int32, (SLOTS, LANES), 0) + shift
    for half in range(2):
        for x in range(2):
            quarter = 2 * x + (core ^ half)
            row = pair[pl.ds(quarter, 1), :]
            column = column_of(row)
            rank = jnp.sum(jnp.where((column == row) & before, 1, 0), axis=0, keepdims=True)
            pick = jnp.where(slot == rank, 1.0, 0.0).astype(jnp.bfloat16)
            at = (half * 2 + x) * SLOTS
            for c in range(3):
                part = gathered[pl.ds(pl.multiple_of(quarter * LANES, LANES), LANES), c * LANES : (c + 1) * LANES]
                high, low = split(jnp.where(column == depth_rows[c], part, 0.0))
                high_t[at : at + SLOTS, c * LANES : (c + 1) * LANES] = dot(pick, high).astype(jnp.bfloat16)
                low_t[at : at + SLOTS, c * LANES : (c + 1) * LANES] = dot(pick, low).astype(jnp.bfloat16)
    depth_columns = jnp.concatenate([column_of(r) for r in depth_rows], axis=0)
    t_high, t_low = high_t[...], low_t[...]
    for y in range(4):
        lanes = orbital[y : y + 1, :]
        for i in range(4):
            panel = integrals[pl.ds(y * 4 + i, 3 * LANES, stride=16), :]
            label = lanes ^ orbital_s[block * 4 + i]
            v_high, v_low = split(jnp.where(depth_columns == label, panel, 0.0))
            total = dot(t_high, v_high) + dot(t_high, v_low) + dot(t_low, v_high)
            for half, out in ((0, keep), (1, send)):
                for x in range(2):
                    at = (half * 2 + x) * SLOTS
                    out[pl.ds((x * 4 + y) * 4 * SLOTS + i, SLOTS, stride=4), :] = total[at : at + SLOTS]


def turn_kernel(arrived, out):
    size = 4 * SLOTS
    for i in range(4):
        rows = []
        for y in range(4):
            rows.append(
                arrived[pl.ds(y * size + i, SLOTS, stride=4), :] + arrived[pl.ds((4 + y) * size + i, SLOTS, stride=4), :]
            )
        out[pl.ds(i, LANES, stride=4), :] = jnp.transpose(jnp.concatenate(rows, axis=0))


def spread_kernel(first, place, slots, labels, orbital_s, orbital, summed, other, swapped, *rest):
    out, turned, packed = rest[-3:]
    block, x, shift = place[0], place[4], place[3]
    size = 4 * SLOTS
    for j in range(4):
        for s in range(32):
            turned[j * LANES + s * 4 : j * LANES + s * 4 + 4, :] = swapped[s * 16 + j * 4 : s * 16 + j * 4 + 4, :]
    for j in range(4):
        mirrored = jnp.transpose(turned[j * LANES : (j + 1) * LANES, :])
        for y in range(4):
            own = summed[pl.ds(x * 4 * size + y * size + j, SLOTS, stride=4), :]
            own = own + other[pl.ds(y * size + j, SLOTS, stride=4), :]
            packed[pl.ds(y * 4 + j, SLOTS, stride=16), :] = own - mirrored[y * SLOTS : (y + 1) * SLOTS]
    rows = []
    for y in range(4):
        for j in range(4):
            rows.append(orbital[y : y + 1, :] ^ orbital_s[block * 4 + j])
    entry = jnp.concatenate(rows, axis=0)

    def step(p, carry):
        slot = slots[p] - shift
        inside = (slot >= 0) & (slot < SLOTS)
        spot = pl.multiple_of(jnp.clip(slot, 0, SLOTS - 1) * 16, 16)
        values = packed[pl.ds(spot, 16), :]
        where = pl.ds(pl.multiple_of(p * 16, 16), 16)
        if first:
            out[where, :] = jnp.where((entry == labels[p]) & inside, values, 0.0)
        else:

            @pl.when(inside)
            def _():
                out[where, :] = jnp.where(entry == labels[p], values, 0.0)

        return carry

    if not first:
        out[...] = rest[0][...]
    lax.fori_loop(0, LANES, step, 0, unroll=4)


def on_device(amplitudes, integrals, orbital_irrep, slab_irrep, pair_irrep):
    y, xh, z = lax.axis_index("y"), lax.axis_index("xh"), lax.axis_index("z")
    x, core = lax.axis_index("xl"), lax.axis_index("core")
    block, occ = (y * 2 + xh) * 16 + z, x * 2 + core
    params = pltpu.CompilerParams(vmem_limit_bytes=40 * 1024 * 1024)

    mine = amplitudes.reshape(4, 384)
    near = lax.all_to_all(jnp.broadcast_to(mine[None], (16, 4, 384)), "z", 0, 0, tiled=True)
    near = jnp.broadcast_to(near.reshape(1, 64, 384), (8, 64, 384))
    gathered = lax.all_to_all(near, ("y", "xh"), 0, 0, tiled=True).reshape(512, 384)

    panel = integrals.reshape(3, LANES, 4, 4, LANES).transpose(0, 1, 3, 2, 4).reshape(3 * LANES * 16, LANES)
    orbital = orbital_irrep.reshape(4, LANES)
    pair = pair_irrep.reshape(4, LANES)
    same = pair[:, :, None] == pair[:, None, :]
    earlier = jnp.arange(LANES)[:, None] < jnp.arange(LANES)[None, :]
    ranks = jnp.sum(same & earlier[None], axis=1, dtype=jnp.int32)
    rounds = jnp.max(ranks) // SLOTS + 1
    slots = lax.dynamic_slice_in_dim(ranks, occ, 1, 0)[0]
    labels = lax.dynamic_slice_in_dim(pair, occ, 1, 0)[0]

    def one_round(turn, previous):
        place = jnp.stack([block, occ, core, turn * SLOTS, x]).astype(jnp.int32)
        keep, send = pl.pallas_call(
            ladder_kernel,
            out_shape=[jax.ShapeDtypeStruct((8 * 4 * SLOTS, LANES), jnp.float32)] * 2,
            in_specs=[SMEM] * 3 + [VMEM] * 4,
            out_specs=[VMEM] * 2,
            scratch_shapes=[pltpu.VMEM((4 * SLOTS, 384), jnp.bfloat16)] * 2,
            compiler_params=params,
            name="ladder",
        )(place, slab_irrep, orbital_irrep, orbital, pair, gathered, panel)
        arrived = lax.ppermute(send, "core", [(0, 1), (1, 0)])
        summed = keep + arrived
        half = 16 * SLOTS
        other = lax.ppermute(lax.dynamic_slice_in_dim(summed, (1 - x) * half, half, 0), "xl", [(0, 1), (1, 0)])
        columns = lax.all_to_all(summed, ("xl", "y"), 0, 0, tiled=True)
        turned = pl.pallas_call(
            turn_kernel,
            out_shape=jax.ShapeDtypeStruct((512, LANES), jnp.float32),
            in_specs=[VMEM],
            out_specs=VMEM,
            compiler_params=params,
            name="turn",
        )(columns)
        swapped = lax.all_to_all(turned, ("xh", "z"), 0, 0, tiled=True)
        first = previous is None
        operands = [place, slots, labels, orbital_irrep, orbital, summed, other, swapped]
        operands += [] if first else [previous]
        return pl.pallas_call(
            functools.partial(spread_kernel, first),
            out_shape=jax.ShapeDtypeStruct((LANES * 16, LANES), jnp.float32),
            in_specs=[SMEM] * 4 + [VMEM] * (len(operands) - 4),
            out_specs=VMEM,
            scratch_shapes=[pltpu.VMEM((512, LANES), jnp.float32), pltpu.VMEM((16 * SLOTS, LANES), jnp.float32)],
            compiler_params=params,
            name="spread",
        )(*operands)

    filled = one_round(jnp.int32(0), None)
    _, filled = lax.while_loop(
        lambda state: state[0] < rounds,
        lambda state: (state[0] + 1, one_round(state[0], state[1])),
        (jnp.int32(1), filled),
    )
    return filled.reshape(LANES, 4, 4, LANES).transpose(0, 2, 1, 3).reshape(LANES, 4, 512)


def solution(mesh):
    devices = np.asarray(mesh.devices).reshape(4, 2, 16, 2, 2)
    fine = Mesh(devices, ("y", "xh", "z", "xl", "core"))
    blocks, groups = ("y", "xh", "z"), ("xl", "core")
    placed = (P(blocks, None, groups), P(None, groups, blocks, None), P(), P(), P())
    return jax.shard_map(
        on_device,
        mesh=fine,
        in_specs=placed,
        out_specs=P(groups, blocks, None),
        check_vma=False,
    )
```

```python
import functools

import jax
import jax.numpy as jnp
import numpy as np
from jax import lax
from jax.experimental import pallas as pl
from jax.experimental.pallas import tpu as pltpu
from jax.sharding import Mesh
from jax.sharding import PartitionSpec as P

SLOTS = 32
LANES = 128
VMEM = pl.BlockSpec(memory_space=pltpu.VMEM)
SMEM = pl.BlockSpec(memory_space=pltpu.SMEM)


def split(x):
    high = x.astype(jnp.bfloat16)
    return high, (x - high.astype(jnp.float32)).astype(jnp.bfloat16)


def dot(x, y):
    return jnp.dot(x, y, preferred_element_type=jnp.float32)


def column_of(row):
    return jnp.transpose(jnp.broadcast_to(row, (LANES, LANES)))


def prepare_kernel(place, slab, orbital_s, orbital, pair, integrals, high, low, columns):
    block, occ = place[0], place[1]
    depth_row = orbital[pl.ds(occ, 1), :]
    depth = jnp.concatenate([column_of(depth_row ^ slab[c]) for c in range(3)], axis=0)
    for y in range(4):
        lanes = orbital[y : y + 1, :]
        for i in range(4):
            panel = integrals[pl.ds(y * 4 + i, 3 * LANES, stride=16), :]
            label = lanes ^ orbital_s[block * 4 + i]
            at = (y * 4 + i) * LANES
            high[:, at : at + LANES], low[:, at : at + LANES] = split(jnp.where(depth == label, panel, 0.0))
    for q in range(4):
        columns[q * LANES : (q + 1) * LANES, :] = column_of(pair[q : q + 1, :])


def ladder_kernel(place, slab, orbital, ranks, columns, gathered, v_high, v_low, keep, send, both_t):
    occ, core, shift = place[1], place[2], place[3]
    depth_row = orbital[pl.ds(occ, 1), :]
    depth_rows = [depth_row ^ slab[c] for c in range(3)]
    slot = lax.broadcasted_iota(jnp.int32, (SLOTS, LANES), 0) + shift
    for half in range(2):
        for x in range(2):
            quarter = 2 * x + (core ^ half)
            pick = jnp.where(slot == ranks[pl.ds(quarter, 1), :], 1.0, 0.0).astype(jnp.bfloat16)
            pairs = pl.ds(pl.multiple_of(quarter * LANES, LANES), LANES)
            column = columns[pairs, :]
            at = (half * 2 + x) * SLOTS
            for c in range(3):
                lanes = slice(c * LANES, (c + 1) * LANES)
                high, low = split(jnp.where(column == depth_rows[c], gathered[pairs, lanes], 0.0))
                both_t[at : at + SLOTS, lanes] = dot(pick, high).astype(jnp.bfloat16)
                both_t[LANES + at : LANES + at + SLOTS, lanes] = dot(pick, low).astype(jnp.bfloat16)
    near = lax.broadcasted_iota(jnp.int32, (LANES, LANES), 1) < 64
    for y in range(4):
        panel = slice(y * 512, (y + 1) * 512)
        parts = dot(both_t[...], v_high[:, panel])
        total = parts[:LANES] + parts[LANES:] + dot(both_t[:LANES, :], v_low[:, panel])
        for m in range(2):
            even, odd = total[:, 2 * m * LANES : (2 * m + 1) * LANES], total[:, (2 * m + 1) * LANES : (2 * m + 2) * LANES]
            cut = (
                jnp.where(near, even, pltpu.roll(odd, 64, 1)),
                jnp.where(near, pltpu.roll(even, 64, 1), odd),
            )
            for half, out in ((0, keep), (1, send)):
                for x in range(2):
                    at = (half * 2 + x) * SLOTS
                    for h in range(2):
                        to = (((x * 4 + y) * 2 + h) * 2 + m) * SLOTS
                        out[to : to + SLOTS, :] = cut[h][at : at + SLOTS]


def turn_kernel(arrived, out, turned):
    for h in range(2):
        for m in range(2):
            rows = []
            for y in range(4):
                at = ((y * 2 + h) * 2 + m) * SLOTS
                rows.append(arrived[at : at + SLOTS, :] + arrived[512 + at : 512 + at + SLOTS, :])
            turned[...] = jnp.transpose(jnp.concatenate(rows, axis=0))
            for e in range(2):
                for j in range(4):
                    out[pl.ds(j * 8 + h * 4 + 2 * m + e, 16, stride=32), :] = turned[pl.ds(e * 64 + j, 16, stride=4), :]


def spread_kernel(first, place, slots, labels, orbital_s, orbital, summed, other, swapped, *rest):
    out, turned, packed = rest[-3:]
    block, x, shift = place[0], place[4], place[3]
    for j in range(4):
        for h in range(2):
            for i in range(4):
                rows = swapped[pl.ds(j * 8 + h * 4 + i, 16, stride=32), :]
                turned[pl.ds(j * LANES + h * 64 + i, 16, stride=4), :] = rows
    mirrored = [jnp.transpose(turned[j * LANES : (j + 1) * LANES, :]) for j in range(4)]
    near = lax.broadcasted_iota(jnp.int32, (SLOTS, LANES), 1) < 64
    for y in range(4):
        for m in range(2):
            cut = []
            for h in range(2):
                at = ((y * 2 + h) * 2 + m) * SLOTS
                cut.append(summed[pl.ds(pl.multiple_of(x * 512 + at, SLOTS), SLOTS), :] + other[at : at + SLOTS, :])
            own = (
                jnp.where(near, cut[0], pltpu.roll(cut[1], 64, 1)),
                jnp.where(near, pltpu.roll(cut[0], 64, 1), cut[1]),
            )
            for e in range(2):
                j = 2 * m + e
                packed[pl.ds(y * 4 + j, SLOTS, stride=16), :] = own[e] - mirrored[j][y * SLOTS : (y + 1) * SLOTS]
    entries = []
    for y in range(4):
        entries.append(jnp.concatenate([orbital[y : y + 1, :] ^ orbital_s[block * 4 + j] for j in range(4)], axis=0))

    def step(p, carry):
        slot = slots[p] - shift
        inside = (slot >= 0) & (slot < SLOTS)
        spot = pl.multiple_of(jnp.clip(slot, 0, SLOTS - 1) * 16, 16)

        def store(wanted):
            for y in range(4):
                values = packed[pl.ds(spot + y * 4, 4), :]
                out[p, :, y * LANES : (y + 1) * LANES] = jnp.where(entries[y] == wanted, values, 0.0)

        if first:
            store(jnp.where(inside, labels[p], -1))
        else:
            pl.when(inside)(lambda: store(labels[p]))
        return carry

    if not first:
        out[...] = rest[0][...]
    lax.fori_loop(0, LANES, step, 0, unroll=4)


def on_device(amplitudes, integrals, orbital_irrep, slab_irrep, pair_irrep):
    y, xh, z = lax.axis_index("y"), lax.axis_index("xh"), lax.axis_index("z")
    x, core = lax.axis_index("xl"), lax.axis_index("core")
    block, occ = (y * 2 + xh) * 16 + z, x * 2 + core
    params = pltpu.CompilerParams(vmem_limit_bytes=40 * 1024 * 1024)

    mine = amplitudes.reshape(4, 384)
    near = lax.all_to_all(jnp.broadcast_to(mine[None], (16, 4, 384)), "z", 0, 0, tiled=True)
    near = jnp.broadcast_to(near.reshape(1, 64, 384), (8, 64, 384))
    gathered = lax.all_to_all(near, ("y", "xh"), 0, 0, tiled=True).reshape(512, 384)

    panel = integrals.reshape(3, LANES, 4, 4, LANES).transpose(0, 1, 3, 2, 4).reshape(3 * LANES * 16, LANES)
    orbital = orbital_irrep.reshape(4, LANES)
    pair = pair_irrep.reshape(4, LANES)
    same = pair[:, :, None] == pair[:, None, :]
    earlier = jnp.arange(LANES)[:, None] < jnp.arange(LANES)[None, :]
    ranks = jnp.sum(same & earlier[None], axis=1, dtype=jnp.int32)
    rounds = jnp.max(ranks) // SLOTS + 1
    slots = lax.dynamic_slice_in_dim(ranks, occ, 1, 0)[0]
    labels = lax.dynamic_slice_in_dim(pair, occ, 1, 0)[0]

    base = jnp.stack([block, occ, core, 0, x]).astype(jnp.int32)
    v_high, v_low, columns = pl.pallas_call(
        prepare_kernel,
        out_shape=[jax.ShapeDtypeStruct((384, 2048), jnp.bfloat16)] * 2 + [jax.ShapeDtypeStruct((512, LANES), jnp.int32)],
        in_specs=[SMEM] * 3 + [VMEM] * 3,
        out_specs=[VMEM] * 3,
        compiler_params=params,
        cost_estimate=pl.CostEstimate(flops=8_000_000, bytes_accessed=7_000_000, transcendentals=0),
        name="prepare",
    )(base, slab_irrep, orbital_irrep, orbital, pair, panel)

    def one_round(turn, previous):
        place = jnp.stack([block, occ, core, turn * SLOTS, x]).astype(jnp.int32)
        keep, send = pl.pallas_call(
            ladder_kernel,
            out_shape=[jax.ShapeDtypeStruct((1024, LANES), jnp.float32)] * 2,
            in_specs=[SMEM] * 2 + [VMEM] * 6,
            out_specs=[VMEM] * 2,
            scratch_shapes=[pltpu.VMEM((2 * LANES, 384), jnp.bfloat16)],
            compiler_params=params,
            name="ladder",
        )(place, slab_irrep, orbital, ranks, columns, gathered, v_high, v_low)
        arrived = lax.ppermute(send, "core", [(0, 1), (1, 0)])
        summed = keep + arrived
        other = lax.ppermute(lax.dynamic_slice_in_dim(summed, (1 - x) * 512, 512, 0), "xl", [(0, 1), (1, 0)])
        traded = lax.all_to_all(summed.reshape(16, 64, LANES), ("xl", "y", "xh"), 0, 0, tiled=True).reshape(1024, LANES)
        traded, other = lax.optimization_barrier((traded, other))
        turned = pl.pallas_call(
            turn_kernel,
            out_shape=jax.ShapeDtypeStruct((512, LANES), jnp.float32),
            in_specs=[VMEM],
            out_specs=VMEM,
            scratch_shapes=[pltpu.VMEM((LANES, LANES), jnp.float32)],
            compiler_params=params,
            name="turn",
        )(traded)
        swapped = lax.all_to_all(turned.reshape(16, 32, LANES), "z", 0, 0, tiled=True).reshape(512, LANES)
        first = previous is None
        operands = [place, slots, labels, orbital_irrep, orbital, summed, other, swapped]
        operands += [] if first else [previous]
        return pl.pallas_call(
            functools.partial(spread_kernel, first),
            out_shape=jax.ShapeDtypeStruct((LANES, 4, 512), jnp.float32),
            in_specs=[SMEM] * 4 + [VMEM] * (len(operands) - 4),
            out_specs=VMEM,
            scratch_shapes=[pltpu.VMEM((512, LANES), jnp.float32), pltpu.VMEM((16 * SLOTS, LANES), jnp.float32)],
            compiler_params=params,
            name="spread",
        )(*operands)

    filled = one_round(jnp.int32(0), None)
    _, filled = lax.while_loop(
        lambda state: state[0] < rounds,
        lambda state: (state[0] + 1, one_round(state[0], state[1])),
        (jnp.int32(1), filled),
    )
    return filled


def solution(mesh):
    devices = np.asarray(mesh.devices).reshape(4, 2, 16, 2, 2)
    fine = Mesh(devices, ("y", "xh", "z", "xl", "core"))
    blocks, groups = ("y", "xh", "z"), ("xl", "core")
    placed = (P(blocks, None, groups), P(None, groups, blocks, None), P(), P(), P())
    return jax.shard_map(
        on_device,
        mesh=fine,
        in_specs=placed,
        out_specs=P(groups, blocks, None),
        check_vma=False,
    )
```

```python
import functools

import jax
import jax.numpy as jnp
import numpy as np
from jax import lax
from jax.experimental import pallas as pl
from jax.experimental.pallas import tpu as pltpu
from jax.sharding import Mesh
from jax.sharding import PartitionSpec as P

LANES = 128
GROUP = 64
SLOTS = 32
KEPT = 24
HALF = 16
DEPTH = 3 * LANES
VMEM = pl.BlockSpec(memory_space=pltpu.VMEM)
SMEM = pl.BlockSpec(memory_space=pltpu.SMEM)


def split(x):
    high = x.astype(jnp.bfloat16)
    return high, (x - high.astype(jnp.float32)).astype(jnp.bfloat16)


def dot(x, y):
    return jnp.dot(x, y, preferred_element_type=jnp.float32)


def iota(shape, dim):
    return lax.broadcasted_iota(jnp.int32, shape, dim)


def column_of(row):
    return jnp.transpose(jnp.broadcast_to(row, (LANES, LANES)))


def plan_kernel(turn, pair, sent, slots, targets, rounds):
    source, lane = iota((LANES, LANES), 0), iota((LANES, LANES), 1)
    near = source < GROUP
    mate = near == (lane < GROUP)
    later = iota((1, LANES), 1) >= GROUP
    ranks, firsts, starts = [], [], []
    most, total = 0, 0
    for q in range(4):
        row = pair[q : q + 1, :]
        column = column_of(row)
        same = column == row

        def count(where):
            return jnp.sum(jnp.where(where, 1, 0), axis=0, keepdims=True)

        ranks.append(count(same & mate & (source < lane)))
        firsts.append(count(same & near))
        most = jnp.maximum(most, jnp.max(count(same & mate)))
        total = jnp.maximum(total, jnp.max(count(same)))
        starts.append([count((column == (lane + t * LANES) // KEPT) & near) for t in range(2)])
    one = (most <= KEPT) & (total <= SLOTS)
    rounds[0] = jnp.where(one, 1, (most + HALF - 1) // HALF)
    shift = turn[0] * HALF
    for q in range(4):
        window = ranks[q] - shift
        window = jnp.where((window >= 0) & (window < HALF), window, -1)
        chosen = jnp.where(one, ranks[q], window)
        base = jnp.where(one, firsts[q], HALF)
        sent[q : q + 1, :] = chosen
        slots[q : q + 1, :] = jnp.where(chosen < 0, -1, chosen + jnp.where(later, base, 0))
        for t in range(2):
            spot = (iota((1, LANES), 1) + t * LANES) % KEPT
            start = jnp.where(one, starts[q][t], HALF)
            targets[q : q + 1, t * LANES : (t + 1) * LANES] = spot + start


def pack_kernel(place, slab, orbital, pair, sent, near, out, column):
    occ, quarter, later = place[1], place[5], place[6]
    depth_row = orbital[pl.ds(occ, 1), :]
    column[...] = column_of(pair[pl.ds(quarter, 1), :])
    mine = pl.ds(pl.multiple_of(later * GROUP, GROUP), GROUP)
    column = column[mine, :]
    chosen = sent[pl.ds(quarter, 1), :]
    chosen = jnp.where(later == 1, pltpu.roll(chosen, GROUP, 1), chosen)[:, :GROUP]
    pick = jnp.where(iota((KEPT, GROUP), 0) == chosen, 1.0, 0.0).astype(jnp.bfloat16)
    for c in range(3):
        lanes = slice(c * LANES, (c + 1) * LANES)
        high, low = split(jnp.where(column == depth_row ^ slab[c], near[:, lanes], 0.0))
        kept = dot(pick, high) + dot(pick, low)
        for to in range(8):
            out[to * KEPT : (to + 1) * KEPT, lanes] = kept


def prepare_kernel(place, slab, orbital_s, orbital, integrals, high, low):
    block, occ = place[0], place[1]
    depth_row = orbital[pl.ds(occ, 1), :]
    depth = jnp.concatenate([column_of(depth_row ^ slab[c]) for c in range(3)], axis=0)
    for y in range(4):
        lanes = orbital[y : y + 1, :]
        for i in range(4):
            panel = integrals[pl.ds(y * 4 + i, DEPTH, stride=16), :]
            label = lanes ^ orbital_s[block * 4 + i]
            at = (y * 4 + i) * LANES
            high[:, at : at + LANES], low[:, at : at + LANES] = split(jnp.where(depth == label, panel, 0.0))


def ladder_kernel(place, slab, orbital, targets, gathered, v_high, v_low, keep, send, both_t):
    occ, core = place[1], place[2]
    depth_row = orbital[pl.ds(occ, 1), :]
    depth_row = jnp.concatenate([depth_row ^ slab[c] for c in range(3)], axis=1)
    slot = iota((SLOTS, 8 * KEPT), 0)
    for half in range(2):
        for x in range(2):
            quarter = 2 * x + (core ^ half)
            pick = jnp.where(slot == targets[pl.ds(quarter, 1), : 8 * KEPT], 1.0, 0.0).astype(jnp.bfloat16)
            at = (half * 2 + x) * SLOTS
            first = gathered[pl.ds(pl.multiple_of(quarter * 2 * KEPT, 8), KEPT), :]
            second = gathered[pl.ds(pl.multiple_of(quarter * 2 * KEPT + KEPT, 8), KEPT), :]
            second = jnp.concatenate([jnp.where(depth_row == l, second, 0.0) for l in range(8)], axis=0)
            first = jnp.concatenate([first, jnp.zeros((SLOTS - KEPT, DEPTH), jnp.float32)], axis=0)
            for to, one, two in zip((at, LANES + at), split(first), split(second)):
                both_t[to : to + SLOTS, :] = (one.astype(jnp.float32) + dot(pick, two)).astype(jnp.bfloat16)
    near = iota((LANES, LANES), 1) < 64
    for y in range(4):
        panel = slice(y * 512, (y + 1) * 512)
        parts = dot(both_t[...], v_high[:, panel])
        total = parts[:LANES] + parts[LANES:] + dot(both_t[:LANES, :], v_low[:, panel])
        for m in range(2):
            even, odd = total[:, 2 * m * LANES : (2 * m + 1) * LANES], total[:, (2 * m + 1) * LANES : (2 * m + 2) * LANES]
            cut = (
                jnp.where(near, even, pltpu.roll(odd, 64, 1)),
                jnp.where(near, pltpu.roll(even, 64, 1), odd),
            )
            for half, out in ((0, keep), (1, send)):
                for x in range(2):
                    at = (half * 2 + x) * SLOTS
                    for h in range(2):
                        to = (((x * 4 + y) * 2 + h) * 2 + m) * SLOTS
                        out[to : to + SLOTS, :] = cut[h][at : at + SLOTS]


def add_kernel(place, keep, arrived, summed, other):
    x = place[4]
    summed[...] = keep[...] + arrived[...]
    other[...] = summed[pl.ds(pl.multiple_of((1 - x) * 512, 512), 512), :]


def turn_kernel(arrived, out, turned):
    for h in range(2):
        for m in range(2):
            rows = []
            for y in range(4):
                at = ((y * 2 + h) * 2 + m) * SLOTS
                rows.append(arrived[at : at + SLOTS, :] + arrived[512 + at : 512 + at + SLOTS, :])
            turned[...] = jnp.transpose(jnp.concatenate(rows, axis=0))
            for e in range(2):
                for j in range(4):
                    out[pl.ds(j * 8 + h * 4 + 2 * m + e, 16, stride=32), :] = turned[pl.ds(e * 64 + j, 16, stride=4), :]


def spread_kernel(first, place, slots, labels, orbital_s, orbital, summed, other, swapped, *rest):
    out, turned, packed = rest[-3:]
    block, x = place[0], place[4]
    for j in range(4):
        for h in range(2):
            for i in range(4):
                rows = swapped[pl.ds(j * 8 + h * 4 + i, 16, stride=32), :]
                turned[pl.ds(j * LANES + h * 64 + i, 16, stride=4), :] = rows
    mirrored = [jnp.transpose(turned[j * LANES : (j + 1) * LANES, :]) for j in range(4)]
    near = iota((SLOTS, LANES), 1) < 64
    for y in range(4):
        for m in range(2):
            cut = []
            for h in range(2):
                at = ((y * 2 + h) * 2 + m) * SLOTS
                cut.append(summed[pl.ds(pl.multiple_of(x * 512 + at, SLOTS), SLOTS), :] + other[at : at + SLOTS, :])
            own = (
                jnp.where(near, cut[0], pltpu.roll(cut[1], 64, 1)),
                jnp.where(near, pltpu.roll(cut[0], 64, 1), cut[1]),
            )
            for e in range(2):
                j = 2 * m + e
                packed[pl.ds(y * 4 + j, SLOTS, stride=16), :] = own[e] - mirrored[j][y * SLOTS : (y + 1) * SLOTS]
    rows = []
    for y in range(4):
        for j in range(4):
            rows.append(orbital[y : y + 1, :] ^ orbital_s[block * 4 + j])
    entry = jnp.concatenate(rows, axis=0)

    def step(p, carry):
        slot = slots[p]
        inside = slot >= 0
        values = packed[pl.ds(pl.multiple_of(jnp.maximum(slot, 0) * 16, 16), 16), :]
        where = pl.ds(pl.multiple_of(p * 16, 16), 16)
        if first:
            out[where, :] = jnp.where(entry == jnp.where(inside, labels[p], -1), values, 0.0)
        else:

            @pl.when(inside)
            def _():
                out[where, :] = jnp.where(entry == labels[p], values, 0.0)

        return carry

    if not first:
        out[...] = rest[0][...]
    lax.fori_loop(0, LANES, step, 0, unroll=8)


def call(kernel, name, scalars, out_shape, operands, scratch=(), cost=None, out_specs=None):
    return pl.pallas_call(
        kernel,
        out_shape=out_shape,
        in_specs=[SMEM] * scalars + [VMEM] * (len(operands) - scalars),
        out_specs=out_specs or jax.tree.map(lambda _: VMEM, out_shape),
        scratch_shapes=list(scratch),
        compiler_params=pltpu.CompilerParams(vmem_limit_bytes=40 * 1024 * 1024),
        cost_estimate=cost and pl.CostEstimate(flops=cost[0], bytes_accessed=cost[1], transcendentals=0),
        name=name,
    )(*operands)


def on_device(amplitudes, integrals, orbital_irrep, slab_irrep, pair_irrep):
    y, xh, z = lax.axis_index("y"), lax.axis_index("xh"), lax.axis_index("z")
    x, core = lax.axis_index("xl"), lax.axis_index("core")
    block, occ = (y * 2 + xh) * 16 + z, x * 2 + core
    place = jnp.stack([block, occ, core, 0, x, y, xh]).astype(jnp.int32)
    f32 = functools.partial(jax.ShapeDtypeStruct, dtype=jnp.float32)
    i32 = functools.partial(jax.ShapeDtypeStruct, dtype=jnp.int32)
    half = jax.ShapeDtypeStruct((DEPTH, 2048), jnp.bfloat16)

    mine = amplitudes.reshape(4, DEPTH)
    near = lax.all_to_all(jnp.broadcast_to(mine[None], (16, 4, DEPTH)), "z", 0, 0, tiled=True).reshape(GROUP, DEPTH)

    panel = integrals.reshape(3, LANES, 4, 4, LANES).transpose(0, 1, 3, 2, 4).reshape(DEPTH * 16, LANES)
    orbital = orbital_irrep.reshape(4, LANES)
    pair = pair_irrep.reshape(4, LANES)
    labels = lax.dynamic_slice_in_dim(pair, occ, 1, 0)[0]
    v_high, v_low = call(
        prepare_kernel,
        "prepare",
        3,
        [half, half],
        [place, slab_irrep, orbital_irrep, orbital, panel],
        cost=(8_000_000, 7_000_000),
    )

    def one_round(turn, previous):
        sent, slots, targets, rounds = call(
            plan_kernel,
            "plan",
            1,
            [i32((4, LANES)), i32((4, LANES)), i32((4, 2 * LANES)), i32((1,))],
            [turn.reshape(1), pair],
            out_specs=[VMEM, VMEM, VMEM, SMEM],
        )
        own_slots = lax.dynamic_slice_in_dim(slots, occ, 1, 0)[0]
        packed = call(
            pack_kernel,
            "pack",
            2,
            f32((8 * KEPT, DEPTH)),
            [place, slab_irrep, orbital, pair, sent, near],
            [pltpu.VMEM((LANES, LANES), jnp.int32)],
        )
        gathered = lax.all_to_all(packed.reshape(8, KEPT, DEPTH), ("y", "xh"), 0, 0, tiled=True).reshape(8 * KEPT, DEPTH)
        keep, send = call(
            ladder_kernel,
            "ladder",
            2,
            [f32((1024, LANES)), f32((1024, LANES))],
            [place, slab_irrep, orbital, targets, gathered, v_high, v_low],
            [pltpu.VMEM((2 * LANES, DEPTH), jnp.bfloat16)],
        )
        arrived = lax.ppermute(send, "core", [(0, 1), (1, 0)])
        summed, other = call(
            add_kernel, "add", 1, [f32((1024, LANES)), f32((512, LANES))], [place, keep, arrived]
        )
        other = lax.ppermute(other, "xl", [(0, 1), (1, 0)])
        traded = lax.all_to_all(summed.reshape(16, GROUP, LANES), ("xl", "y", "xh"), 0, 0, tiled=True)
        turned = call(
            turn_kernel,
            "turn",
            0,
            f32((512, LANES)),
            [traded.reshape(1024, LANES)],
            [pltpu.VMEM((LANES, LANES), jnp.float32)],
        )
        swapped = lax.all_to_all(turned.reshape(16, 32, LANES), "z", 0, 0, tiled=True).reshape(512, LANES)
        first = previous is None
        operands = [place, own_slots, labels, orbital_irrep, orbital, summed, other, swapped]
        if not first:
            operands.append(previous.reshape(LANES, 4, 4, LANES).transpose(0, 2, 1, 3).reshape(2048, LANES))
        filled = call(
            functools.partial(spread_kernel, first),
            "spread",
            4,
            f32((2048, LANES)),
            operands,
            [pltpu.VMEM((512, LANES), jnp.float32), pltpu.VMEM((16 * SLOTS, LANES), jnp.float32)],
        )
        return filled.reshape(LANES, 4, 4, LANES).transpose(0, 2, 1, 3).reshape(LANES, 4, 512), rounds[0]

    filled, rounds = one_round(jnp.int32(0), None)
    _, filled = lax.while_loop(
        lambda state: state[0] < rounds,
        lambda state: (state[0] + 1, one_round(state[0], state[1])[0]),
        (jnp.int32(1), filled),
    )
    return filled


def solution(mesh):
    devices = np.asarray(mesh.devices).reshape(4, 2, 16, 2, 2)
    fine = Mesh(devices, ("y", "xh", "z", "xl", "core"))
    blocks, groups = ("y", "xh", "z"), ("xl", "core")
    placed = (P(blocks, None, groups), P(None, groups, blocks, None), P(), P(), P())
    return jax.shard_map(
        on_device,
        mesh=fine,
        in_specs=placed,
        out_specs=P(groups, blocks, None),
        check_vma=False,
    )
```

```python
import functools

import jax
import jax.numpy as jnp
import numpy as np
from jax import lax
from jax.experimental import pallas as pl
from jax.experimental.pallas import tpu as pltpu
from jax.sharding import Mesh
from jax.sharding import PartitionSpec as P

LANES = 128
GROUP = 64
SLOTS = 32
KEPT = 24
HALF = 16
DEPTH = 3 * LANES
VMEM = pl.BlockSpec(memory_space=pltpu.VMEM)
SMEM = pl.BlockSpec(memory_space=pltpu.SMEM)
ANY = pl.BlockSpec(memory_space=pl.ANY)


def split(x):
    high = x.astype(jnp.bfloat16)
    return high, (x - high.astype(jnp.float32)).astype(jnp.bfloat16)


def dot(x, y):
    return jnp.dot(x, y, preferred_element_type=jnp.float32)


def iota(shape, dim):
    return lax.broadcasted_iota(jnp.int32, shape, dim)


def column_of(row):
    return jnp.transpose(jnp.broadcast_to(row, (LANES, LANES)))


def plan_kernel(turn, place, pair, sent, slots, targets, mates, rounds, column_s):
    source, lane = iota((LANES, LANES), 0), iota((LANES, LANES), 1)
    near = source < GROUP
    mate = near == (lane < GROUP)
    later = iota((1, LANES), 1) >= GROUP
    ranks, firsts, starts = [], [], []
    most, total = 0, 0
    for q in range(4):
        row = pair[q : q + 1, :]
        column = column_of(row)
        same = column == row

        def count(where):
            return jnp.sum(jnp.where(where, 1, 0), axis=0, keepdims=True)

        ranks.append(count(same & mate & (source < lane)))
        firsts.append(count(same & near))
        most = jnp.maximum(most, jnp.max(count(same & mate)))
        total = jnp.maximum(total, jnp.max(count(same)))
        starts.append([count((column == (lane + t * LANES) // KEPT) & near) for t in range(2)])
    one = (most <= KEPT) & (total <= SLOTS)
    rounds[0] = jnp.where(one, 1, (most + HALF - 1) // HALF)
    shift = turn[0] * HALF
    for q in range(4):
        window = ranks[q] - shift
        window = jnp.where((window >= 0) & (window < HALF), window, -1)
        chosen = jnp.where(one, ranks[q], window)
        base = jnp.where(one, firsts[q], HALF)
        sent[q : q + 1, :] = chosen
        slots[q : q + 1, :] = jnp.where(chosen < 0, -1, chosen + jnp.where(later, base, 0))
        for t in range(2):
            spot = (iota((1, LANES), 1) + t * LANES) % KEPT
            start = jnp.where(one, starts[q][t], HALF)
            targets[q : q + 1, t * LANES : (t + 1) * LANES] = spot + start
    column_s[...] = column_of(pair[pl.ds(place[5], 1), :])
    mates[...] = column_s[pl.ds(pl.multiple_of(place[6] * GROUP, GROUP), GROUP), :]


def pack_kernel(place, slab, orbital, mates, sent, near, out):
    occ, quarter, later = place[1], place[5], place[6]
    depth_row = orbital[pl.ds(occ, 1), :]
    column = mates[...]
    chosen = sent[pl.ds(quarter, 1), :]
    chosen = jnp.where(later == 1, pltpu.roll(chosen, GROUP, 1), chosen)[:, :GROUP]
    pick = jnp.where(iota((KEPT, GROUP), 0) == chosen, 1.0, 0.0).astype(jnp.bfloat16)
    for c in range(3):
        lanes = slice(c * LANES, (c + 1) * LANES)
        high, low = split(jnp.where(column == depth_row ^ slab[c], near[:, lanes], 0.0))
        kept = dot(pick, high) + dot(pick, low)
        for to in range(8):
            out[to * KEPT : (to + 1) * KEPT, lanes] = kept


def prepare_kernel(place, slab, orbital_s, orbital, integrals, high, low):
    block, occ = place[0], place[1]
    depth_row = orbital[pl.ds(occ, 1), :]
    depth = jnp.concatenate([column_of(depth_row ^ slab[c]) for c in range(3)], axis=0)
    for y in range(4):
        lanes = orbital[y : y + 1, :]
        for i in range(4):
            panel = integrals[pl.ds(y * 4 + i, DEPTH, stride=16), :]
            label = lanes ^ orbital_s[block * 4 + i]
            at = (y * 4 + i) * LANES
            high[:, at : at + LANES], low[:, at : at + LANES] = split(jnp.where(depth == label, panel, 0.0))


def ladder_kernel(place, slab, orbital, targets, gathered, v_high, v_low, keep, send, both_t):
    occ, core = place[1], place[2]
    depth_row = orbital[pl.ds(occ, 1), :]
    depth_row = jnp.concatenate([depth_row ^ slab[c] for c in range(3)], axis=1)
    slot = iota((SLOTS, 8 * KEPT), 0)
    for half in range(2):
        for x in range(2):
            quarter = 2 * x + (core ^ half)
            pick = jnp.where(slot == targets[pl.ds(quarter, 1), : 8 * KEPT], 1.0, 0.0).astype(jnp.bfloat16)
            at = (half * 2 + x) * SLOTS
            first = gathered[pl.ds(pl.multiple_of(quarter * 2 * KEPT, 8), KEPT), :]
            second = gathered[pl.ds(pl.multiple_of(quarter * 2 * KEPT + KEPT, 8), KEPT), :]
            second = jnp.concatenate([jnp.where(depth_row == l, second, 0.0) for l in range(8)], axis=0)
            first = jnp.concatenate([first, jnp.zeros((SLOTS - KEPT, DEPTH), jnp.float32)], axis=0)
            for to, one, two in zip((at, LANES + at), split(first), split(second)):
                both_t[to : to + SLOTS, :] = (one.astype(jnp.float32) + dot(pick, two)).astype(jnp.bfloat16)
    near = iota((LANES, LANES), 1) < 64
    for y in range(4):
        panel = slice(y * 512, (y + 1) * 512)
        parts = dot(both_t[...], v_high[:, panel])
        total = parts[:LANES] + parts[LANES:] + dot(both_t[:LANES, :], v_low[:, panel])
        for m in range(2):
            even, odd = total[:, 2 * m * LANES : (2 * m + 1) * LANES], total[:, (2 * m + 1) * LANES : (2 * m + 2) * LANES]
            cut = (
                jnp.where(near, even, pltpu.roll(odd, 64, 1)),
                jnp.where(near, pltpu.roll(even, 64, 1), odd),
            )
            for half, out in ((0, keep), (1, send)):
                for x in range(2):
                    at = (half * 2 + x) * SLOTS
                    for h in range(2):
                        to = (((x * 4 + y) * 2 + h) * 2 + m) * SLOTS
                        out[to : to + SLOTS, :] = cut[h][at : at + SLOTS]


def add_kernel(place, keep, arrived, summed, other):
    x = place[4]
    summed[...] = keep[...] + arrived[...]
    other[...] = summed[pl.ds(pl.multiple_of((1 - x) * 512, 512), 512), :]


def turn_kernel(arrived, out, turned):
    for h in range(2):
        for m in range(2):
            rows = []
            for y in range(4):
                at = ((y * 2 + h) * 2 + m) * SLOTS
                rows.append(arrived[at : at + SLOTS, :] + arrived[512 + at : 512 + at + SLOTS, :])
            turned[...] = jnp.transpose(jnp.concatenate(rows, axis=0))
            for e in range(2):
                for j in range(4):
                    out[pl.ds(j * 8 + h * 4 + 2 * m + e, 16, stride=32), :] = turned[pl.ds(e * 64 + j, 16, stride=4), :]


def spread_kernel(
    place, rounds, slots, labels, orbital_s, orbital, summed, other, swapped, previous, out, turned, packed, filled, done
):
    block, x = place[0], place[4]
    several = rounds[0] > 1
    for j in range(4):
        for h in range(2):
            for i in range(4):
                rows = swapped[pl.ds(j * 8 + h * 4 + i, 16, stride=32), :]
                turned[pl.ds(j * LANES + h * 64 + i, 16, stride=4), :] = rows
    mirrored = [jnp.transpose(turned[j * LANES : (j + 1) * LANES, :]) for j in range(4)]
    near = iota((SLOTS, LANES), 1) < 64
    for y in range(4):
        for m in range(2):
            cut = []
            for h in range(2):
                at = ((y * 2 + h) * 2 + m) * SLOTS
                cut.append(summed[pl.ds(pl.multiple_of(x * 512 + at, SLOTS), SLOTS), :] + other[at : at + SLOTS, :])
            own = (
                jnp.where(near, cut[0], pltpu.roll(cut[1], 64, 1)),
                jnp.where(near, pltpu.roll(cut[0], 64, 1), cut[1]),
            )
            for e in range(2):
                j = 2 * m + e
                packed[pl.ds(y * 4 + j, SLOTS, stride=16), :] = own[e] - mirrored[j][y * SLOTS : (y + 1) * SLOTS]
    rows = []
    for y in range(4):
        for j in range(4):
            rows.append(orbital[y : y + 1, :] ^ orbital_s[block * 4 + j])
    entry = jnp.concatenate(rows, axis=0)

    def rows_of(p):
        return pl.ds(pl.multiple_of(p * 16, 16), 16)

    def store(p, slot):
        values = packed[pl.ds(pl.multiple_of(slot * 16, 16), 16), :]
        filled[rows_of(p), :] = jnp.where(entry == labels[p], values, 0.0)

    def part_of(part):
        return pltpu.make_async_copy(filled.at[pl.ds(part * 512, 512), :], out.at[pl.ds(part * 512, 512), :], done.at[part])

    @pl.when(several)
    def _():
        copy = pltpu.make_async_copy(previous, filled, done.at[0])
        copy.start()
        copy.wait()

        def step(p, carry):
            pl.when(slots[p] >= 0)(lambda: store(p, slots[p]))
            return carry

        lax.fori_loop(0, LANES, step, 0)
        for part in range(4):
            part_of(part).start()

    @pl.when(jnp.logical_not(several))
    def _():
        def step(p, carry):
            store(p, slots[p])
            return carry

        for part in range(4):
            lax.fori_loop(part * 32, part * 32 + 32, step, 0, unroll=8)
            part_of(part).start()

    for part in range(4):
        part_of(part).wait()


def call(kernel, name, scalars, out_shape, operands, scratch=(), cost=None, out_specs=None, vmem=8, last=VMEM):
    return pl.pallas_call(
        kernel,
        out_shape=out_shape,
        in_specs=[SMEM] * scalars + [VMEM] * (len(operands) - scalars - 1) + [last],
        out_specs=out_specs or jax.tree.map(lambda _: VMEM, out_shape),
        scratch_shapes=list(scratch),
        compiler_params=pltpu.CompilerParams(vmem_limit_bytes=vmem * 1024 * 1024),
        cost_estimate=cost and pl.CostEstimate(flops=cost[0], bytes_accessed=cost[1], transcendentals=0),
        name=name,
    )(*operands)


def on_device(amplitudes, integrals, orbital_irrep, slab_irrep, pair_irrep):
    y, xh, z = lax.axis_index("y"), lax.axis_index("xh"), lax.axis_index("z")
    x, core = lax.axis_index("xl"), lax.axis_index("core")
    block, occ = (y * 2 + xh) * 16 + z, x * 2 + core
    place = jnp.stack([block, occ, core, 0, x, y, xh]).astype(jnp.int32)
    f32 = functools.partial(jax.ShapeDtypeStruct, dtype=jnp.float32)
    i32 = functools.partial(jax.ShapeDtypeStruct, dtype=jnp.int32)
    half = jax.ShapeDtypeStruct((DEPTH, 2048), jnp.bfloat16)

    mine = amplitudes.reshape(4, DEPTH)
    near = lax.all_to_all(jnp.broadcast_to(mine[None], (16, 4, DEPTH)), "z", 0, 0, tiled=True).reshape(GROUP, DEPTH)

    panel = integrals.reshape(3, LANES, 4, 4, LANES).transpose(0, 1, 3, 2, 4).reshape(DEPTH * 16, LANES)
    orbital = orbital_irrep.reshape(4, LANES)
    pair = pair_irrep.reshape(4, LANES)
    labels = lax.dynamic_slice_in_dim(pair, occ, 1, 0)[0]
    v_high, v_low = call(
        prepare_kernel,
        "prepare",
        3,
        [half, half],
        [place, slab_irrep, orbital_irrep, orbital, panel],
        cost=(8_000_000, 7_000_000),
        vmem=16,
    )
    near, v_high, v_low = lax.optimization_barrier((near, v_high, v_low))

    def one_round(turn):
        sent, slots, targets, mates, rounds = call(
            plan_kernel,
            "plan",
            2,
            [i32((4, LANES)), i32((4, LANES)), i32((4, 2 * LANES)), i32((GROUP, LANES)), i32((1,))],
            [turn.reshape(1), place, pair],
            [pltpu.VMEM((LANES, LANES), jnp.int32)],
            out_specs=[VMEM, VMEM, VMEM, VMEM, SMEM],
        )
        own_slots = lax.dynamic_slice_in_dim(slots, occ, 1, 0)[0]
        packed = call(
            pack_kernel,
            "pack",
            2,
            f32((8 * KEPT, DEPTH)),
            [place, slab_irrep, orbital, mates, sent, near],
        )
        gathered = lax.all_to_all(packed.reshape(8, KEPT, DEPTH), ("y", "xh"), 0, 0, tiled=True).reshape(8 * KEPT, DEPTH)
        keep, send = call(
            ladder_kernel,
            "ladder",
            2,
            [f32((1024, LANES)), f32((1024, LANES))],
            [place, slab_irrep, orbital, targets, gathered, v_high, v_low],
            [pltpu.VMEM((2 * LANES, DEPTH), jnp.bfloat16)],
            vmem=16,
        )
        arrived = lax.ppermute(send, "core", [(0, 1), (1, 0)])
        summed, other = call(
            add_kernel, "add", 1, [f32((1024, LANES)), f32((512, LANES))], [place, keep, arrived]
        )
        other = lax.ppermute(other, "xl", [(0, 1), (1, 0)])
        traded = lax.all_to_all(summed.reshape(16, GROUP, LANES), ("xl", "y", "xh"), 0, 0, tiled=True)
        turned = call(
            turn_kernel,
            "turn",
            0,
            f32((512, LANES)),
            [traded.reshape(1024, LANES)],
            [pltpu.VMEM((LANES, LANES), jnp.float32)],
        )
        swapped = lax.all_to_all(turned.reshape(16, 32, LANES), "z", 0, 0, tiled=True).reshape(512, LANES)
        return rounds, own_slots, summed, other, swapped

    def spread(previous, rounds, own_slots, summed, other, swapped):
        return call(
            spread_kernel,
            "spread",
            5,
            f32((2048, LANES)),
            [place, rounds, own_slots, labels, orbital_irrep, orbital, summed, other, swapped, previous],
            [
                pltpu.VMEM((512, LANES), jnp.float32),
                pltpu.VMEM((16 * SLOTS, LANES), jnp.float32),
                pltpu.VMEM((2048, LANES), jnp.float32),
                pltpu.SemaphoreType.DMA((4,)),
            ],
            out_specs=ANY,
            last=ANY,
        )

    rounds, own_slots, summed, other, swapped = one_round(jnp.int32(0))
    empty = jnp.zeros((2048, LANES), jnp.float32)
    empty, summed, other, swapped = lax.optimization_barrier((empty, summed, other, swapped))
    _, previous = lax.while_loop(
        lambda state: state[0] < rounds[0],
        lambda state: (state[0] + 1, spread(state[1], *one_round(state[0]))),
        (jnp.int32(1), empty),
    )
    filled = spread(previous, rounds, own_slots, summed, other, swapped)
    return filled.reshape(LANES, 4, 4, LANES).transpose(0, 2, 1, 3).reshape(LANES, 4, 512)


def solution(mesh):
    devices = np.asarray(mesh.devices).reshape(4, 2, 16, 2, 2)
    fine = Mesh(devices, ("y", "xh", "z", "xl", "core"))
    blocks, groups = ("y", "xh", "z"), ("xl", "core")
    placed = (P(blocks, None, groups), P(None, groups, blocks, None), P(), P(), P())
    return jax.shard_map(
        on_device,
        mesh=fine,
        in_specs=placed,
        out_specs=P(groups, blocks, None),
        check_vma=False,
    )
```

```python
import functools

import jax
import jax.numpy as jnp
import numpy as np
from jax import lax
from jax.experimental import pallas as pl
from jax.experimental.pallas import tpu as pltpu
from jax.sharding import Mesh
from jax.sharding import PartitionSpec as P

LANES = 128
GROUP = 64
SLOTS = 32
KEPT = 24
HALF = 16
DEPTH = 3 * LANES
VMEM = pl.BlockSpec(memory_space=pltpu.VMEM)
SMEM = pl.BlockSpec(memory_space=pltpu.SMEM)
ANY = pl.BlockSpec(memory_space=pl.ANY)


def split(x):
    high = x.astype(jnp.bfloat16)
    return high, (x - high.astype(jnp.float32)).astype(jnp.bfloat16)


def dot(x, y):
    return jnp.dot(x, y, preferred_element_type=jnp.float32)


def iota(shape, dim):
    return lax.broadcasted_iota(jnp.int32, shape, dim)


def count(where):
    return jnp.sum(jnp.where(where, 1, 0), axis=0, keepdims=True)


def column_of(row):
    return jnp.transpose(jnp.broadcast_to(row, (LANES, LANES)))


def plan_kernel(turn, pair, slots, targets, rounds):
    source, lane = iota((LANES, LANES), 0), iota((LANES, LANES), 1)
    near = source < GROUP
    mate = near == (lane < GROUP)
    later = iota((1, LANES), 1) >= GROUP
    ranks, firsts, starts = [], [], []
    most, total = 0, 0
    for q in range(4):
        row = pair[q : q + 1, :]
        column = column_of(row)
        same = column == row
        ranks.append(count(same & mate & (source < lane)))
        firsts.append(count(same & near))
        most = jnp.maximum(most, jnp.max(count(same & mate)))
        total = jnp.maximum(total, jnp.max(count(same)))
        starts.append([count((column == (lane + t * LANES) // KEPT) & near) for t in range(2)])
    one = (most <= KEPT) & (total <= SLOTS)
    rounds[0] = jnp.where(one, 1, (most + HALF - 1) // HALF)
    shift = turn[0] * HALF
    for q in range(4):
        window = ranks[q] - shift
        window = jnp.where((window >= 0) & (window < HALF), window, -1)
        chosen = jnp.where(one, ranks[q], window)
        base = jnp.where(one, firsts[q], HALF)
        slots[q : q + 1, :] = jnp.where(chosen < 0, -1, chosen + jnp.where(later, base, 0))
        for t in range(2):
            spot = (iota((1, LANES), 1) + t * LANES) % KEPT
            split_up = jnp.where(spot < HALF, spot + HALF, -1)
            targets[q : q + 1, t * LANES : (t + 1) * LANES] = jnp.where(one, spot + starts[q][t], split_up)


def pack_kernel(turn, place, slab, orbital, pair, near, out, column_s):
    occ, quarter, later = place[1], place[5], place[6]
    depth_row = orbital[pl.ds(occ, 1), :]
    row = pair[pl.ds(quarter, 1), :]
    column = column_of(row)
    column_s[...] = column
    source, lane = iota((LANES, LANES), 0), iota((LANES, LANES), 1)
    mate = (source < GROUP) == (lane < GROUP)
    chosen = count((column == row) & mate & (source < lane)) - turn[0] * HALF
    chosen = jnp.where(later == 1, pltpu.roll(chosen, GROUP, 1), chosen)[:, :GROUP]
    pick = jnp.where(iota((KEPT, GROUP), 0) == chosen, 1.0, 0.0).astype(jnp.bfloat16)
    column = column_s[pl.ds(pl.multiple_of(later * GROUP, GROUP), GROUP), :]
    for c in range(3):
        lanes = slice(c * LANES, (c + 1) * LANES)
        high, low = split(jnp.where(column == depth_row ^ slab[c], near[:, lanes], 0.0))
        kept = dot(pick, high) + dot(pick, low)
        for to in range(8):
            out[to * KEPT : (to + 1) * KEPT, lanes] = kept


def prepare_kernel(place, slab, orbital_s, orbital, integrals, high, low):
    block, occ = place[0], place[1]
    depth_row = orbital[pl.ds(occ, 1), :]
    depth = jnp.concatenate([column_of(depth_row ^ slab[c]) for c in range(3)], axis=0)
    for y in range(4):
        lanes = orbital[y : y + 1, :]
        for i in range(4):
            panel = integrals[pl.ds(y * 4 + i, DEPTH, stride=16), :]
            label = lanes ^ orbital_s[block * 4 + i]
            at = (y * 4 + i) * LANES
            high[:, at : at + LANES], low[:, at : at + LANES] = split(jnp.where(depth == label, panel, 0.0))


def ladder_kernel(place, slab, rounds, orbital, targets, gathered, v_high, v_low, keep, send, both_t):
    occ, core = place[1], place[2]
    depth_row = orbital[pl.ds(occ, 1), :]
    depth_row = jnp.concatenate([depth_row ^ slab[c] for c in range(3)], axis=1)
    slot = iota((SLOTS, 8 * KEPT), 0)
    kept = jnp.where(rounds[0] > 1, HALF, KEPT)
    for half in range(2):
        for x in range(2):
            quarter = 2 * x + (core ^ half)
            pick = jnp.where(slot == targets[pl.ds(quarter, 1), : 8 * KEPT], 1.0, 0.0).astype(jnp.bfloat16)
            at = (half * 2 + x) * SLOTS
            first = gathered[pl.ds(pl.multiple_of(quarter * 2 * KEPT, 8), KEPT), :]
            second = gathered[pl.ds(pl.multiple_of(quarter * 2 * KEPT + KEPT, 8), KEPT), :]
            second = jnp.concatenate([jnp.where(depth_row == l, second, 0.0) for l in range(8)], axis=0)
            first = jnp.where(iota((KEPT, DEPTH), 0) < kept, first, 0.0)
            first = jnp.concatenate([first, jnp.zeros((SLOTS - KEPT, DEPTH), jnp.float32)], axis=0)
            for to, one, two in zip((at, LANES + at), split(first), split(second)):
                both_t[to : to + SLOTS, :] = (one.astype(jnp.float32) + dot(pick, two)).astype(jnp.bfloat16)
    near = iota((LANES, LANES), 1) < 64
    for y in range(4):
        panel = slice(y * 512, (y + 1) * 512)
        parts = dot(both_t[...], v_high[:, panel])
        total = parts[:LANES] + parts[LANES:] + dot(both_t[:LANES, :], v_low[:, panel])
        for m in range(2):
            even, odd = total[:, 2 * m * LANES : (2 * m + 1) * LANES], total[:, (2 * m + 1) * LANES : (2 * m + 2) * LANES]
            cut = (
                jnp.where(near, even, pltpu.roll(odd, 64, 1)),
                jnp.where(near, pltpu.roll(even, 64, 1), odd),
            )
            for half, out in ((0, keep), (1, send)):
                for x in range(2):
                    at = (half * 2 + x) * SLOTS
                    for h in range(2):
                        to = (((y * 2 + h) * 2 + x) * 2 + m) * SLOTS
                        out[to : to + SLOTS, :] = cut[h][at : at + SLOTS]


def add_kernel(place, keep, arrived, summed, other):
    x = place[4]
    summed[...] = keep[...] + arrived[...]
    for block in range(8):
        rows = pl.ds(pl.multiple_of((block * 2 + 1 - x) * GROUP, GROUP), GROUP)
        other[block * GROUP : (block + 1) * GROUP, :] = summed[rows, :]


def turn_kernel(arrived, out, turned):
    for h in range(2):
        for m in range(2):
            rows = []
            for y in range(4):
                at = (y * 2 + h) * 2 * GROUP + m * SLOTS
                rows.append(arrived[at : at + SLOTS, :] + arrived[GROUP + at : GROUP + at + SLOTS, :])
            turned[...] = jnp.transpose(jnp.concatenate(rows, axis=0))
            for e in range(2):
                for j in range(4):
                    out[pl.ds(j * 8 + h * 4 + 2 * m + e, 16, stride=32), :] = turned[pl.ds(e * 64 + j, 16, stride=4), :]


def spread_kernel(
    place, rounds, slots, labels, orbital_s, orbital, summed, other, swapped, previous, out, turned, packed, filled, done
):
    block, x = place[0], place[4]
    several = rounds[0] > 1
    for j in range(4):
        for h in range(2):
            for i in range(4):
                rows = swapped[pl.ds(j * 8 + h * 4 + i, 16, stride=32), :]
                turned[pl.ds(j * LANES + h * 64 + i, 16, stride=4), :] = rows
    mirrored = [jnp.transpose(turned[j * LANES : (j + 1) * LANES, :]) for j in range(4)]
    near = iota((SLOTS, LANES), 1) < 64
    for y in range(4):
        for m in range(2):
            cut = []
            for h in range(2):
                at = (y * 2 + h) * GROUP + m * SLOTS
                mine = ((y * 2 + h) * 2 + x) * GROUP + m * SLOTS
                cut.append(summed[pl.ds(pl.multiple_of(mine, SLOTS), SLOTS), :] + other[at : at + SLOTS, :])
            own = (
                jnp.where(near, cut[0], pltpu.roll(cut[1], 64, 1)),
                jnp.where(near, pltpu.roll(cut[0], 64, 1), cut[1]),
            )
            for e in range(2):
                j = 2 * m + e
                packed[pl.ds(y * 4 + j, SLOTS, stride=16), :] = own[e] - mirrored[j][y * SLOTS : (y + 1) * SLOTS]
    rows = []
    for y in range(4):
        for j in range(4):
            rows.append(orbital[y : y + 1, :] ^ orbital_s[block * 4 + j])
    entry = jnp.concatenate(rows, axis=0)

    def rows_of(p):
        return pl.ds(pl.multiple_of(p * 16, 16), 16)

    def store(p, slot):
        values = packed[pl.ds(pl.multiple_of(slot * 16, 16), 16), :]
        filled[rows_of(p), :] = jnp.where(entry == labels[p], values, 0.0)

    def part_of(part):
        return pltpu.make_async_copy(filled.at[pl.ds(part * 512, 512), :], out.at[pl.ds(part * 512, 512), :], done.at[part])

    @pl.when(several)
    def _():
        copy = pltpu.make_async_copy(previous, filled, done.at[0])
        copy.start()
        copy.wait()

        def step(p, carry):
            pl.when(slots[p] >= 0)(lambda: store(p, slots[p]))
            return carry

        lax.fori_loop(0, LANES, step, 0)
        for part in range(4):
            part_of(part).start()

    @pl.when(jnp.logical_not(several))
    def _():
        def step(p, carry):
            store(p, slots[p])
            return carry

        for part in range(4):
            lax.fori_loop(part * 32, part * 32 + 32, step, 0, unroll=8)
            part_of(part).start()

    for part in range(4):
        part_of(part).wait()


def call(kernel, name, scalars, out_shape, operands, scratch=(), cost=None, out_specs=None, vmem=8, last=VMEM):
    return pl.pallas_call(
        kernel,
        out_shape=out_shape,
        in_specs=[SMEM] * scalars + [VMEM] * (len(operands) - scalars - 1) + [last],
        out_specs=out_specs or jax.tree.map(lambda _: VMEM, out_shape),
        scratch_shapes=list(scratch),
        compiler_params=pltpu.CompilerParams(vmem_limit_bytes=vmem * 1024 * 1024),
        cost_estimate=cost and pl.CostEstimate(flops=cost[0], bytes_accessed=cost[1], transcendentals=0),
        name=name,
    )(*operands)


def on_device(amplitudes, integrals, orbital_irrep, slab_irrep, pair_irrep):
    y, xh, z = lax.axis_index("y"), lax.axis_index("xh"), lax.axis_index("z")
    x, core = lax.axis_index("xl"), lax.axis_index("core")
    block, occ = (y * 2 + xh) * 16 + z, x * 2 + core
    place = jnp.stack([block, occ, core, 0, x, y, xh]).astype(jnp.int32)
    f32 = functools.partial(jax.ShapeDtypeStruct, dtype=jnp.float32)
    i32 = functools.partial(jax.ShapeDtypeStruct, dtype=jnp.int32)
    half = jax.ShapeDtypeStruct((DEPTH, 2048), jnp.bfloat16)

    mine = amplitudes.reshape(4, DEPTH)
    near = lax.all_to_all(jnp.broadcast_to(mine[None], (16, 4, DEPTH)), "z", 0, 0, tiled=True).reshape(GROUP, DEPTH)

    panel = integrals.reshape(3, LANES, 4, 4, LANES).transpose(0, 1, 3, 2, 4).reshape(DEPTH * 16, LANES)
    orbital = orbital_irrep.reshape(4, LANES)
    pair = pair_irrep.reshape(4, LANES)
    labels = lax.dynamic_slice_in_dim(pair, occ, 1, 0)[0]

    near, late_pair, late_place = lax.optimization_barrier((near, pair, place))

    def one_round(turn, near):
        turn = turn.reshape(1)
        packed = call(
            pack_kernel,
            "pack",
            3,
            f32((8 * KEPT, DEPTH)),
            [turn, place, slab_irrep, orbital, pair, near],
            [pltpu.VMEM((LANES, LANES), jnp.int32)],
        )
        gathered = lax.all_to_all(packed.reshape(8, KEPT, DEPTH), ("y", "xh"), 0, 0, tiled=True).reshape(8 * KEPT, DEPTH)
        slots, targets, rounds = call(
            plan_kernel,
            "plan",
            1,
            [i32((4, LANES)), i32((4, 2 * LANES)), i32((1,))],
            [turn, late_pair],
            out_specs=[VMEM, VMEM, SMEM],
        )
        v_high, v_low = call(
            prepare_kernel,
            "prepare",
            3,
            [half, half],
            [late_place, slab_irrep, orbital_irrep, orbital, panel],
            cost=(8_000_000, 7_000_000),
            vmem=16,
        )
        own_slots = lax.dynamic_slice_in_dim(slots, occ, 1, 0)[0]
        keep, send = call(
            ladder_kernel,
            "ladder",
            3,
            [f32((1024, LANES)), f32((1024, LANES))],
            [place, slab_irrep, rounds, orbital, targets, gathered, v_high, v_low],
            [pltpu.VMEM((2 * LANES, DEPTH), jnp.bfloat16)],
            vmem=16,
        )
        arrived = lax.ppermute(send, "core", [(0, 1), (1, 0)])
        summed, other = call(
            add_kernel, "add", 1, [f32((1024, LANES)), f32((512, LANES))], [place, keep, arrived]
        )
        other = lax.ppermute(other, "xl", [(0, 1), (1, 0)])
        traded = lax.all_to_all(summed.reshape(16, GROUP, LANES), ("y", "xh", "xl"), 0, 0, tiled=True)
        turned = call(
            turn_kernel,
            "turn",
            0,
            f32((512, LANES)),
            [traded.reshape(1024, LANES)],
            [pltpu.VMEM((LANES, LANES), jnp.float32)],
        )
        empty = jnp.zeros((2048, LANES), jnp.float32)
        turned, other, summed, own_slots, rounds, empty = lax.optimization_barrier(
            (turned, other, summed, own_slots, rounds, empty)
        )
        swapped = lax.all_to_all(turned.reshape(16, 32, LANES), "z", 0, 0, tiled=True).reshape(512, LANES)
        return rounds, own_slots, summed, other, swapped, empty

    def spread(previous, rounds, own_slots, summed, other, swapped):
        return call(
            spread_kernel,
            "spread",
            5,
            f32((2048, LANES)),
            [place, rounds, own_slots, labels, orbital_irrep, orbital, summed, other, swapped, previous],
            [
                pltpu.VMEM((512, LANES), jnp.float32),
                pltpu.VMEM((16 * SLOTS, LANES), jnp.float32),
                pltpu.VMEM((2048, LANES), jnp.float32),
                pltpu.SemaphoreType.DMA((4,)),
            ],
            out_specs=ANY,
            last=ANY,
        )

    rounds, own_slots, summed, other, swapped, empty = one_round(jnp.int32(0), near)
    empty, summed, other, swapped = lax.optimization_barrier((empty, summed, other, swapped))
    _, previous = lax.while_loop(
        lambda state: state[0] < rounds[0],
        lambda state: (state[0] + 1, spread(state[1], *one_round(state[0], near)[:-1])),
        (jnp.int32(1), empty),
    )
    filled = spread(previous, rounds, own_slots, summed, other, swapped)
    return filled.reshape(LANES, 4, 4, LANES).transpose(0, 2, 1, 3).reshape(LANES, 4, 512)


def solution(mesh):
    devices = np.asarray(mesh.devices).reshape(4, 2, 16, 2, 2)
    fine = Mesh(devices, ("y", "xh", "z", "xl", "core"))
    blocks, groups = ("y", "xh", "z"), ("xl", "core")
    placed = (P(blocks, None, groups), P(None, groups, blocks, None), P(), P(), P())
    return jax.shard_map(
        on_device,
        mesh=fine,
        in_specs=placed,
        out_specs=P(groups, blocks, None),
        check_vma=False,
    )
```

```python
import functools

import jax
import jax.numpy as jnp
import numpy as np
from jax import lax
from jax.experimental import pallas as pl
from jax.experimental.pallas import tpu as pltpu
from jax.sharding import Mesh
from jax.sharding import PartitionSpec as P

LANES = 128
GROUP = 64
SLOTS = 32
FEW = 24
KEPT = 24
HALF = 16
DEPTH = 3 * LANES
VMEM = pl.BlockSpec(memory_space=pltpu.VMEM)
SMEM = pl.BlockSpec(memory_space=pltpu.SMEM)
HBM = pl.BlockSpec(memory_space=pltpu.HBM)


def split(x):
    high = x.astype(jnp.bfloat16)
    return high, (x - high.astype(jnp.float32)).astype(jnp.bfloat16)


def dot(x, y):
    return jnp.dot(x, y, preferred_element_type=jnp.float32)


def iota(shape, dim):
    return lax.broadcasted_iota(jnp.int32, shape, dim)


def count(where):
    return jnp.sum(jnp.where(where, 1, 0), axis=0, keepdims=True)


def column_of(row):
    return jnp.transpose(jnp.broadcast_to(row, (LANES, LANES)))


def plan_kernel(turn, place, pair, sent, slots, targets, mates, rounds, column_s):
    source, lane = iota((LANES, LANES), 0), iota((LANES, LANES), 1)
    near = source < GROUP
    mate = near == (lane < GROUP)
    later = iota((1, LANES), 1) >= GROUP
    ranks, firsts, starts = [], [], []
    most, total = 0, 0
    for q in range(4):
        row = pair[q : q + 1, :]
        column = column_of(row)
        same = column == row

        ranks.append(count(same & mate & (source < lane)))
        firsts.append(count(same & near))
        most = jnp.maximum(most, jnp.max(count(same & mate)))
        total = jnp.maximum(total, jnp.max(count(same)))
        starts.append([count((column == (lane + t * LANES) // KEPT) & near) for t in range(2)])
    one = (most <= KEPT) & (total <= SLOTS)
    rounds[0] = jnp.where(one, 1, (most + HALF - 1) // HALF)
    rounds[1] = jnp.where(total <= FEW, 1, 0)
    shift = turn[0] * HALF
    for q in range(4):
        window = ranks[q] - shift
        window = jnp.where((window >= 0) & (window < HALF), window, -1)
        chosen = jnp.where(one, ranks[q], window)
        base = jnp.where(one, firsts[q], HALF)
        sent[q : q + 1, :] = chosen
        slots[q : q + 1, :] = jnp.where(chosen < 0, -1, chosen + jnp.where(later, base, 0))
        for t in range(2):
            spot = (iota((1, LANES), 1) + t * LANES) % KEPT
            start = jnp.where(one, starts[q][t], HALF)
            targets[q : q + 1, t * LANES : (t + 1) * LANES] = spot + start
    column_s[...] = column_of(pair[pl.ds(place[5], 1), :])
    mates[...] = column_s[pl.ds(pl.multiple_of(place[6] * GROUP, GROUP), GROUP), :]


def pack_kernel(place, slab, orbital, mates, sent, near, out):
    occ, quarter, later = place[1], place[5], place[6]
    depth_row = orbital[pl.ds(occ, 1), :]
    column = mates[...]
    chosen = sent[pl.ds(quarter, 1), :]
    chosen = jnp.where(later == 1, pltpu.roll(chosen, GROUP, 1), chosen)[:, :GROUP]
    pick = jnp.where(iota((KEPT, GROUP), 0) == chosen, 1.0, 0.0).astype(jnp.bfloat16)
    for c in range(3):
        lanes = slice(c * LANES, (c + 1) * LANES)
        high, low = split(jnp.where(column == depth_row ^ slab[c], near[:, lanes], 0.0))
        kept = dot(pick, high) + dot(pick, low)
        for to in range(8):
            out[to * KEPT : (to + 1) * KEPT, lanes] = kept


def prepare_kernel(place, slab, orbital_s, orbital, integrals, v_high, v_low, panels, high, low, done):
    block, occ = place[0], place[1]
    depth_row = orbital[pl.ds(occ, 1), :]

    def part_of(c):
        rows = pl.ds(c * LANES * 16, LANES * 16)
        return pltpu.make_async_copy(integrals.at[rows, :], panels.at[rows, :], done.at[c])

    def results_of(c):
        rows = pl.ds(c * LANES, LANES)
        yield pltpu.make_async_copy(high.at[rows, :], v_high.at[rows, :], done.at[3 + 2 * c])
        yield pltpu.make_async_copy(low.at[rows, :], v_low.at[rows, :], done.at[4 + 2 * c])

    for c in range(3):
        part_of(c).start()
    for c in range(3):
        depth = column_of(depth_row ^ slab[c])
        part_of(c).wait()
        for y in range(4):
            lanes = orbital[y : y + 1, :]
            for i in range(4):
                panel = panels[pl.ds(c * LANES * 16 + y * 4 + i, LANES, stride=16), :]
                label = lanes ^ orbital_s[block * 4 + i]
                parts = split(jnp.where(depth == label, panel, 0.0))
                columns = slice((y * 4 + i) * LANES, (y * 4 + i + 1) * LANES)
                high[c * LANES : (c + 1) * LANES, columns], low[c * LANES : (c + 1) * LANES, columns] = parts
        for copy in results_of(c):
            copy.start()
    for c in range(3):
        for copy in results_of(c):
            copy.wait()


def ladder_kernel(size, place, slab, orbital, targets, gathered, v_high, v_low, keep, send):
    occ, core = place[1], place[2]
    depth_row = orbital[pl.ds(occ, 1), :]
    depth_row = jnp.concatenate([depth_row ^ slab[c] for c in range(3)], axis=1)
    slot = iota((size, 8 * KEPT), 0)
    highs, lows = [], []
    for half in range(2):
        for x in range(2):
            quarter = 2 * x + (core ^ half)
            pick = jnp.where(slot == targets[pl.ds(quarter, 1), : 8 * KEPT], 1.0, 0.0).astype(jnp.bfloat16)
            first = gathered[pl.ds(pl.multiple_of(quarter * 2 * KEPT, 8), KEPT), :]
            second = gathered[pl.ds(pl.multiple_of(quarter * 2 * KEPT + KEPT, 8), KEPT), :]
            second = jnp.concatenate([jnp.where(depth_row == l, second, 0.0) for l in range(8)], axis=0)
            if size > KEPT:
                first = jnp.concatenate([first, jnp.zeros((size - KEPT, DEPTH), jnp.float32)], axis=0)
            for to, one, two in zip((highs, lows), split(first), split(second)):
                to.append(one.astype(jnp.float32) + dot(pick, two))
    t_both = jnp.concatenate(highs + lows, axis=0).astype(jnp.bfloat16)
    t_high = jnp.concatenate(highs, axis=0).astype(jnp.bfloat16)
    near = iota((4 * size, LANES), 1) < 64
    for y in range(4):
        panel = slice(y * 512, (y + 1) * 512)
        parts = dot(t_both, v_high[:, panel])
        total = parts[: 4 * size] + parts[4 * size :] + dot(t_high, v_low[:, panel])
        for m in range(2):
            even, odd = total[:, 2 * m * LANES : (2 * m + 1) * LANES], total[:, (2 * m + 1) * LANES : (2 * m + 2) * LANES]
            cut = (
                jnp.where(near, even, pltpu.roll(odd, 64, 1)),
                jnp.where(near, pltpu.roll(even, 64, 1), odd),
            )
            for half, out in ((0, keep), (1, send)):
                for x in range(2):
                    at = (half * 2 + x) * size
                    for h in range(2):
                        to = (((y * 2 + h) * 2 + x) * 2 + m) * size
                        out[to : to + size, :] = cut[h][at : at + size]


def add_kernel(size, place, keep, arrived, summed, other):
    x = place[4]
    summed[...] = keep[...] + arrived[...]
    for block in range(8):
        rows = pl.ds(pl.multiple_of((block * 2 + 1 - x) * 2 * size, 8), 2 * size)
        other[block * 2 * size : (block + 1) * 2 * size, :] = summed[rows, :]


def turn_kernel(size, arrived, out, turned):
    lane = iota((16, LANES), 1)
    for h in range(2):
        for m in range(2):
            rows = []
            for y in range(4):
                at = (y * 2 + h) * 4 * size + m * size
                rows.append(arrived[at : at + size, :] + arrived[2 * size + at : 2 * size + at + size, :])
            if size < SLOTS:
                rows.append(jnp.zeros((LANES - 4 * size, LANES), jnp.float32))
            turned[...] = jnp.transpose(jnp.concatenate(rows, axis=0))
            for e in range(2):
                parts = [turned[pl.ds(e * 64 + j, 16, stride=4), :] for j in range(4)]
                if size < SLOTS:
                    last = parts.pop()
                    parts = [jnp.where(lane < 96, part, pltpu.roll(last, 96 - 32 * u, 1)) for u, part in enumerate(parts)]
                for j, part in enumerate(parts):
                    out[pl.ds(j * 8 + h * 4 + 2 * m + e, 16, stride=size), :] = part


def spread_kernel(size, place, rounds, slots, labels, orbital_s, orbital, summed, other, swapped, *rest):
    *rest, turned, packed, filled, done = rest
    held, outs = (rest[:2], rest[2:]) if size == SLOTS else ((), rest)
    block, occ, x = place[0], place[1], place[4]
    lane = iota((16, LANES), 1)
    for h in range(2):
        for i in range(4):
            parts = [swapped[pl.ds(j * 8 + h * 4 + i, 16, stride=size), :] for j in range(size // 8)]
            if size < SLOTS:
                low = jnp.where(lane < 32, pltpu.roll(parts[0], 32, 1), pltpu.roll(parts[1], 64, 1))
                parts.append(jnp.where(lane < 64, low, pltpu.roll(parts[2], 96, 1)))
            for j, part in enumerate(parts):
                turned[pl.ds(j * LANES + h * 64 + i, 16, stride=4), :] = part
    mirrored = [jnp.transpose(turned[j * LANES : (j + 1) * LANES, :]) for j in range(4)]
    near = iota((size, LANES), 1) < 64
    for y in range(4):
        for m in range(2):
            cut = []
            for h in range(2):
                at = (y * 2 + h) * 2 * size + m * size
                mine = ((y * 2 + h) * 2 + x) * 2 * size + m * size
                cut.append(summed[pl.ds(pl.multiple_of(mine, 8), size), :] + other[at : at + size, :])
            own = (
                jnp.where(near, cut[0], pltpu.roll(cut[1], 64, 1)),
                jnp.where(near, pltpu.roll(cut[0], 64, 1), cut[1]),
            )
            for e in range(2):
                j = 2 * m + e
                packed[pl.ds(y * 4 + j, size, stride=16), :] = own[e] - mirrored[j][y * size : (y + 1) * size]
    rows = []
    for y in range(4):
        for j in range(4):
            rows.append(orbital[y : y + 1, :] ^ orbital_s[block * 4 + j])
    entry = jnp.concatenate(rows, axis=0)

    def rows_of(p):
        return pl.ds(pl.multiple_of(p * 16, 16), 16)

    def store(p):
        values = packed[pl.ds(pl.multiple_of(slots[occ, p] * 16, 16), 16), :]
        filled[rows_of(p), :] = jnp.where(entry == labels[occ * LANES + p], values, 0.0)

    def part_of(part):
        share = 4 // len(outs)
        to = outs[part // share].at[pl.ds(part % share * 512, 512), :]
        return pltpu.make_async_copy(filled.at[pl.ds(part * 512, 512), :], to, done.at[part])

    def fill():
        def step(p, carry):
            store(p)
            return carry

        for part in range(4):
            lax.fori_loop(part * 32, part * 32 + 32, step, 0, unroll=8)
            part_of(part).start()

    def fill_in():
        for half in range(2):
            copy = pltpu.make_async_copy(held[half], filled.at[pl.ds(half * 1024, 1024), :], done.at[half])
            copy.start()
            copy.wait()

        def step(p, carry):
            pl.when(slots[occ, p] >= 0)(lambda: store(p))
            return carry

        lax.fori_loop(0, LANES, step, 0)
        for part in range(4):
            part_of(part).start()

    if held:
        pl.when(rounds[0] > 1)(fill_in)
        pl.when(rounds[0] <= 1)(fill)
    else:
        fill()
    for part in range(4):
        part_of(part).wait()


def call(kernel, name, scalars, out_shape, operands, scratch=(), cost=None, out_specs=None, vmem=8, any_last=0):
    return pl.pallas_call(
        kernel,
        out_shape=out_shape,
        in_specs=[SMEM] * scalars + [VMEM] * (len(operands) - scalars - any_last) + [HBM] * any_last,
        out_specs=out_specs or jax.tree.map(lambda _: VMEM, out_shape),
        scratch_shapes=list(scratch),
        compiler_params=pltpu.CompilerParams(vmem_limit_bytes=vmem * 1024 * 1024),
        cost_estimate=cost and pl.CostEstimate(flops=cost[0], bytes_accessed=cost[1], transcendentals=0),
        name=name,
    )(*operands)


def on_device(amplitudes, integrals, orbital_irrep, slab_irrep, pair_irrep):
    y, xh, z = lax.axis_index("y"), lax.axis_index("xh"), lax.axis_index("z")
    x, core = lax.axis_index("xl"), lax.axis_index("core")
    block, occ = (y * 2 + xh) * 16 + z, x * 2 + core
    place = jnp.stack([block, occ, core, 0, x, y, xh]).astype(jnp.int32)
    f32 = functools.partial(jax.ShapeDtypeStruct, dtype=jnp.float32)
    i32 = functools.partial(jax.ShapeDtypeStruct, dtype=jnp.int32)
    half = jax.ShapeDtypeStruct((DEPTH, 2048), jnp.bfloat16)

    mine = jnp.broadcast_to(amplitudes.reshape(1, 4, DEPTH), (16, 4, DEPTH))
    near = lax.all_to_all(mine, "z", 0, 0, tiled=True).reshape(GROUP, DEPTH)

    panel = integrals.reshape(3, LANES, 4, 4, LANES).transpose(0, 1, 3, 2, 4).reshape(DEPTH * 16, LANES)
    orbital = orbital_irrep.reshape(4, LANES)
    pair = pair_irrep.reshape(4, LANES)

    v_high, v_low = call(
        prepare_kernel,
        "prepare",
        3,
        [half, half],
        [place, slab_irrep, orbital_irrep, orbital, panel],
        [
            pltpu.VMEM((DEPTH * 16, LANES), jnp.float32),
            pltpu.VMEM((DEPTH, 2048), jnp.bfloat16),
            pltpu.VMEM((DEPTH, 2048), jnp.bfloat16),
            pltpu.SemaphoreType.DMA((9,)),
        ],
        cost=(8_000_000, 7_000_000),
        out_specs=[HBM, HBM],
        vmem=58,
        any_last=1,
    )

    def plan(turn):
        return call(
            plan_kernel,
            "plan",
            2,
            [i32((4, LANES)), i32((4, LANES)), i32((4, 2 * LANES)), i32((GROUP, LANES)), i32((2,))],
            [turn.reshape(1), place, pair],
            [pltpu.VMEM((LANES, LANES), jnp.int32)],
            out_specs=[VMEM, VMEM, VMEM, VMEM, SMEM],
        )

    def gather(sent, mates):
        packed = call(
            pack_kernel,
            "pack",
            2,
            f32((8 * KEPT, DEPTH)),
            [place, slab_irrep, orbital, mates, sent, near],
        )
        packed = packed.reshape(8, KEPT, DEPTH)
        return lax.all_to_all(packed, ("y", "xh"), 0, 0, tiled=True).reshape(8 * KEPT, DEPTH)

    def work(size, targets, gathered):
        keep, send = call(
            functools.partial(ladder_kernel, size),
            "ladder",
            2,
            [f32((32 * size, LANES))] * 2,
            [place, slab_irrep, orbital, targets, gathered, v_high, v_low],
            vmem=16,
        )
        arrived = lax.ppermute(send, "core", [(0, 1), (1, 0)])
        summed, other = call(
            functools.partial(add_kernel, size),
            "add",
            1,
            [f32((32 * size, LANES)), f32((16 * size, LANES))],
            [place, keep, arrived],
        )
        other = lax.ppermute(other, "xl", [(0, 1), (1, 0)])
        traded = lax.all_to_all(summed.reshape(16, 2 * size, LANES), ("y", "xh", "xl"), 0, 0, tiled=True)
        turned = call(
            functools.partial(turn_kernel, size),
            "turn",
            0,
            f32((16 * size, LANES)),
            [traded.reshape(32 * size, LANES)],
            [pltpu.VMEM((LANES, LANES), jnp.float32)],
        )
        swapped = lax.all_to_all(turned.reshape(16, size, LANES), "z", 0, 0, tiled=True).reshape(16 * size, LANES)
        return (summed, other, swapped), (keep, arrived)

    def spread(size, out_shape, rounds, slots, found, held=()):
        return call(
            functools.partial(spread_kernel, size),
            "spread",
            5,
            out_shape,
            [place, rounds, slots, pair_irrep, orbital_irrep, orbital, *found, *held],
            [
                pltpu.VMEM((512, LANES), jnp.float32),
                pltpu.VMEM((16 * size, LANES), jnp.float32),
                pltpu.VMEM((2048, LANES), jnp.float32),
                pltpu.SemaphoreType.DMA((4,)),
            ],
            out_specs=jax.tree.map(lambda _: HBM, out_shape),
            any_last=len(held),
        )

    sent, slots, targets, mates, rounds = plan(jnp.int32(0))
    near, v_high, v_low, sent, mates = lax.optimization_barrier((near, v_high, v_low, sent, mates))
    gathered = gather(sent, mates)

    def unpacked(filled):
        return filled.reshape(LANES, 4, 4, LANES).transpose(0, 2, 1, 3).reshape(LANES, 4, 512)

    def few(targets, gathered):
        found, _ = work(FEW, targets, gathered)
        return unpacked(spread(FEW, f32((2048, LANES)), rounds, slots, found))

    def many(targets, gathered):
        found, spare = work(SLOTS, targets, gathered)

        def later(state):
            turn, held = state
            sent, slots, targets, mates, _ = plan(turn)
            found, _ = work(SLOTS, targets, gather(sent, mates))
            return turn + 1, tuple(spread(SLOTS, [f32((1024, LANES))] * 2, rounds, slots, found, held))

        found, spare, turn = lax.optimization_barrier((found, spare, jnp.int32(1)))
        _, held = lax.while_loop(lambda state: state[0] < rounds[0], later, (turn, spare))
        return unpacked(spread(SLOTS, f32((2048, LANES)), rounds, slots, found, held))

    return lax.cond(rounds[1] > 0, few, many, targets, gathered)


def solution(mesh):
    devices = np.asarray(mesh.devices).reshape(4, 2, 16, 2, 2)
    fine = Mesh(devices, ("y", "xh", "z", "xl", "core"))
    blocks, groups = ("y", "xh", "z"), ("xl", "core")
    placed = (P(blocks, None, groups), P(None, groups, blocks, None), P(), P(), P())
    return jax.shard_map(
        on_device,
        mesh=fine,
        in_specs=placed,
        out_specs=P(groups, blocks, None),
        check_vma=False,
    )
```

```python
import functools

import jax
import jax.numpy as jnp
import numpy as np
from jax import lax
from jax.experimental import pallas as pl
from jax.experimental.pallas import tpu as pltpu
from jax.sharding import Mesh
from jax.sharding import PartitionSpec as P

LANES = 128
GROUP = 64
SLOTS = 32
FEWER = (24, 28)
KEPT = 24
HALF = 16
DEPTH = 3 * LANES
VMEM = pl.BlockSpec(memory_space=pltpu.VMEM)
SMEM = pl.BlockSpec(memory_space=pltpu.SMEM)
HBM = pl.BlockSpec(memory_space=pltpu.HBM)


def split(x):
    high = x.astype(jnp.bfloat16)
    return high, (x - high.astype(jnp.float32)).astype(jnp.bfloat16)


def dot(x, y):
    return jnp.dot(x, y, preferred_element_type=jnp.float32)


def iota(shape, dim):
    return lax.broadcasted_iota(jnp.int32, shape, dim)


def count(where):
    return jnp.sum(jnp.where(where, 1, 0), axis=0, keepdims=True)


def column_of(row):
    return jnp.transpose(jnp.broadcast_to(row, (LANES, LANES)))


def plan_kernel(turn, place, pair, sent, slots, targets, mates, rounds, choice, column_s):
    source, lane = iota((LANES, LANES), 0), iota((LANES, LANES), 1)
    near = source < GROUP
    mate = near == (lane < GROUP)
    later = iota((1, LANES), 1) >= GROUP
    ranks, firsts, starts = [], [], []
    most, total = 0, 0
    for q in range(4):
        row = pair[q : q + 1, :]
        column = column_of(row)
        same = column == row

        ranks.append(count(same & mate & (source < lane)))
        firsts.append(count(same & near))
        most = jnp.maximum(most, jnp.max(count(same & mate)))
        total = jnp.maximum(total, jnp.max(count(same)))
        starts.append([count((column == (lane + t * LANES) // KEPT) & near) for t in range(2)])
    one = (most <= KEPT) & (total <= SLOTS)
    rounds[0] = jnp.where(one, 1, (most + HALF - 1) // HALF)
    fewer = jnp.where(total <= FEWER[0], 0, jnp.where(total <= FEWER[1], 1, 2))
    choice[0] = jnp.where(one, fewer, 2)
    shift = turn[0] * HALF
    for q in range(4):
        window = ranks[q] - shift
        window = jnp.where((window >= 0) & (window < HALF), window, -1)
        chosen = jnp.where(one, ranks[q], window)
        base = jnp.where(one, firsts[q], HALF)
        sent[q : q + 1, :] = chosen
        slots[q : q + 1, :] = jnp.where(chosen < 0, -1, chosen + jnp.where(later, base, 0))
        for t in range(2):
            spot = (iota((1, LANES), 1) + t * LANES) % KEPT
            start = jnp.where(one, starts[q][t], HALF)
            targets[q : q + 1, t * LANES : (t + 1) * LANES] = spot + start
    column_s[...] = column_of(pair[pl.ds(place[5], 1), :])
    mates[...] = column_s[pl.ds(pl.multiple_of(place[6] * GROUP, GROUP), GROUP), :]


def pack_kernel(place, slab, orbital, mates, sent, near, out):
    occ, quarter, later = place[1], place[5], place[6]
    depth_row = orbital[pl.ds(occ, 1), :]
    column = mates[...]
    chosen = sent[pl.ds(quarter, 1), :]
    chosen = jnp.where(later == 1, pltpu.roll(chosen, GROUP, 1), chosen)[:, :GROUP]
    pick = jnp.where(iota((KEPT, GROUP), 0) == chosen, 1.0, 0.0).astype(jnp.bfloat16)
    for c in range(3):
        lanes = slice(c * LANES, (c + 1) * LANES)
        high, low = split(jnp.where(column == depth_row ^ slab[c], near[:, lanes], 0.0))
        kept = dot(pick, high) + dot(pick, low)
        for to in range(8):
            out[to * KEPT : (to + 1) * KEPT, lanes] = kept


def prepare_kernel(place, slab, orbital_s, orbital, integrals, v_high, v_low, panels, high, low, done):
    block, occ = place[0], place[1]
    depth_row = orbital[pl.ds(occ, 1), :]

    def part_of(c):
        rows = pl.ds(c * LANES * 16, LANES * 16)
        return pltpu.make_async_copy(integrals.at[rows, :], panels.at[rows, :], done.at[c])

    def results_of(c):
        rows = pl.ds(c * LANES, LANES)
        yield pltpu.make_async_copy(high.at[rows, :], v_high.at[rows, :], done.at[3 + 2 * c])
        yield pltpu.make_async_copy(low.at[rows, :], v_low.at[rows, :], done.at[4 + 2 * c])

    for c in range(3):
        part_of(c).start()
    for c in range(3):
        depth = column_of(depth_row ^ slab[c])
        part_of(c).wait()
        for y in range(4):
            lanes = orbital[y : y + 1, :]
            for i in range(4):
                panel = panels[pl.ds(c * LANES * 16 + y * 4 + i, LANES, stride=16), :]
                label = lanes ^ orbital_s[block * 4 + i]
                parts = split(jnp.where(depth == label, panel, 0.0))
                columns = slice((y * 4 + i) * LANES, (y * 4 + i + 1) * LANES)
                high[c * LANES : (c + 1) * LANES, columns], low[c * LANES : (c + 1) * LANES, columns] = parts
        for copy in results_of(c):
            copy.start()
    for c in range(3):
        for copy in results_of(c):
            copy.wait()


def ladder_kernel(size, place, slab, orbital, targets, gathered, v_high, v_low, keep, send):
    occ, core = place[1], place[2]
    depth_row = orbital[pl.ds(occ, 1), :]
    depth_row = jnp.concatenate([depth_row ^ slab[c] for c in range(3)], axis=1)
    width = -(-size // 8) * 8
    slot = iota((width, 8 * KEPT), 0)
    highs, lows = [], []
    for half in range(2):
        for x in range(2):
            quarter = 2 * x + (core ^ half)
            pick = jnp.where(slot == targets[pl.ds(quarter, 1), : 8 * KEPT], 1.0, 0.0).astype(jnp.bfloat16)
            first = gathered[pl.ds(pl.multiple_of(quarter * 2 * KEPT, 8), KEPT), :]
            second = gathered[pl.ds(pl.multiple_of(quarter * 2 * KEPT + KEPT, 8), KEPT), :]
            second = jnp.concatenate([jnp.where(depth_row == l, second, 0.0) for l in range(8)], axis=0)
            if width > KEPT:
                first = jnp.concatenate([first, jnp.zeros((width - KEPT, DEPTH), jnp.float32)], axis=0)
            for to, one, two in zip((highs, lows), split(first), split(second)):
                to.append(one.astype(jnp.float32) + dot(pick, two))
    rows = 4 * width
    t_both = jnp.concatenate(highs + lows, axis=0).astype(jnp.bfloat16)
    t_high = jnp.concatenate(highs, axis=0).astype(jnp.bfloat16)
    near = iota((rows, LANES), 1) < 64
    for y in range(4):
        panel = slice(y * 512, (y + 1) * 512)
        parts = dot(t_both, v_high[:, panel])
        total = parts[:rows] + parts[rows:] + dot(t_high, v_low[:, panel])
        for m in range(2):
            even, odd = total[:, 2 * m * LANES : (2 * m + 1) * LANES], total[:, (2 * m + 1) * LANES : (2 * m + 2) * LANES]
            cut = (
                jnp.where(near, even, pltpu.roll(odd, 64, 1)),
                jnp.where(near, pltpu.roll(even, 64, 1), odd),
            )
            for half, out in ((0, keep), (1, send)):
                for x in range(2):
                    at = (half * 2 + x) * width
                    for h in range(2):
                        to = (((y * 2 + h) * 2 + x) * 2 + m) * size
                        out[to : to + size, :] = cut[h][at : at + size]


def add_kernel(size, place, keep, arrived, summed, other):
    x = place[4]
    summed[...] = keep[...] + arrived[...]
    for block in range(8):
        rows = pl.ds(pl.multiple_of((block * 2 + 1 - x) * 2 * size, 8), 2 * size)
        other[block * 2 * size : (block + 1) * 2 * size, :] = summed[rows, :]


def folded(size):
    spare, gap = LANES - 4 * size, SLOTS - size
    for t in range(gap):
        yield size + t, [(u * gap + t, spare * u) for u in range(size // gap)]


def turn_kernel(size, arrived, out, turned):
    lane = iota((16, LANES), 1)
    for h in range(2):
        for m in range(2):
            rows = []
            for y in range(4):
                at = (y * 2 + h) * 4 * size + m * size
                rows.append(arrived[at : at + size, :] + arrived[2 * size + at : 2 * size + at + size, :])
            if size < SLOTS:
                rows.append(jnp.zeros((LANES - 4 * size, LANES), jnp.float32))
            at = (h * 2 + m) * LANES
            turned[at : at + LANES, :] = jnp.transpose(jnp.concatenate(rows, axis=0))
    parts = []
    for j in range(4):
        for h in range(2):
            for i in range(4):
                parts.append(turned[pl.ds((h * 2 + i // 2) * LANES + i % 2 * 64 + j, 16, stride=4), :])
    for last, pieces in folded(size):
        for row, at in pieces:
            parts[row] = jnp.where(lane < 4 * size, parts[row], pltpu.roll(parts[last], 4 * size - at, 1))
    for row in range(size):
        out[pl.ds(row, 16, stride=size), :] = parts[row]


def spread_kernel(size, place, rounds, slots, labels, orbital_s, orbital, summed, other, swapped, *rest):
    *rest, turned, packed, filled, done = rest
    held, outs = (rest[:2], rest[2:]) if size == SLOTS else ((), rest)
    block, occ, x = place[0], place[1], place[4]
    lane = iota((16, LANES), 1)
    parts = [swapped[pl.ds(row, 16, stride=size), :] for row in range(size)]
    for last, pieces in folded(size):
        whole = None
        for row, at in pieces:
            piece = pltpu.roll(parts[row], (at - 4 * size) % LANES, 1)
            whole = piece if whole is None else jnp.where(lane < at, whole, piece)
        parts.append(whole)
    for j in range(4):
        for h in range(2):
            for i in range(4):
                turned[pl.ds(j * LANES + h * 64 + i, 16, stride=4), :] = parts[j * 8 + h * 4 + i]
    mirrored = [jnp.transpose(turned[j * LANES : (j + 1) * LANES, :]) for j in range(4)]
    near = iota((size, LANES), 1) < 64
    for y in range(4):
        for m in range(2):
            cut = []
            for h in range(2):
                at = (y * 2 + h) * 2 * size + m * size
                mine = summed[pl.ds(pl.multiple_of(((y * 2 + h) * 2 + x) * 2 * size, 8), 2 * size), :]
                cut.append(mine[m * size : (m + 1) * size] + other[at : at + size, :])
            own = (
                jnp.where(near, cut[0], pltpu.roll(cut[1], 64, 1)),
                jnp.where(near, pltpu.roll(cut[0], 64, 1), cut[1]),
            )
            for e in range(2):
                j = 2 * m + e
                packed[pl.ds(y * 4 + j, size, stride=16), :] = own[e] - mirrored[j][y * size : (y + 1) * size]
    rows = []
    for y in range(4):
        for j in range(4):
            rows.append(orbital[y : y + 1, :] ^ orbital_s[block * 4 + j])
    entry = jnp.concatenate(rows, axis=0)

    def rows_of(p):
        return pl.ds(pl.multiple_of(p * 16, 16), 16)

    def store(p):
        values = packed[pl.ds(pl.multiple_of(slots[occ, p] * 16, 16), 16), :]
        filled[rows_of(p), :] = jnp.where(entry == labels[occ * LANES + p], values, 0.0)

    def part_of(part):
        share = 4 // len(outs)
        to = outs[part // share].at[pl.ds(part % share * 512, 512), :]
        return pltpu.make_async_copy(filled.at[pl.ds(part * 512, 512), :], to, done.at[part])

    def fill():
        def step(p, carry):
            store(p)
            return carry

        for part in range(4):
            lax.fori_loop(part * 32, part * 32 + 32, step, 0, unroll=8)
            part_of(part).start()

    def fill_in():
        for half in range(2):
            copy = pltpu.make_async_copy(held[half], filled.at[pl.ds(half * 1024, 1024), :], done.at[half])
            copy.start()
            copy.wait()

        def step(p, carry):
            pl.when(slots[occ, p] >= 0)(lambda: store(p))
            return carry

        lax.fori_loop(0, LANES, step, 0)
        for part in range(4):
            part_of(part).start()

    if held:
        pl.when(rounds[0] > 1)(fill_in)
        pl.when(rounds[0] <= 1)(fill)
    else:
        fill()
    for part in range(4):
        part_of(part).wait()


def call(kernel, name, scalars, out_shape, operands, scratch=(), cost=None, out_specs=None, vmem=8, any_last=0):
    return pl.pallas_call(
        kernel,
        out_shape=out_shape,
        in_specs=[SMEM] * scalars + [VMEM] * (len(operands) - scalars - any_last) + [HBM] * any_last,
        out_specs=out_specs or jax.tree.map(lambda _: VMEM, out_shape),
        scratch_shapes=list(scratch),
        compiler_params=pltpu.CompilerParams(vmem_limit_bytes=vmem * 1024 * 1024),
        cost_estimate=cost and pl.CostEstimate(flops=cost[0], bytes_accessed=cost[1], transcendentals=0),
        name=name,
    )(*operands)


def on_device(amplitudes, integrals, orbital_irrep, slab_irrep, pair_irrep):
    y, xh, z = lax.axis_index("y"), lax.axis_index("xh"), lax.axis_index("z")
    x, core = lax.axis_index("xl"), lax.axis_index("core")
    block, occ = (y * 2 + xh) * 16 + z, x * 2 + core
    place = jnp.stack([block, occ, core, 0, x, y, xh]).astype(jnp.int32)
    f32 = functools.partial(jax.ShapeDtypeStruct, dtype=jnp.float32)
    i32 = functools.partial(jax.ShapeDtypeStruct, dtype=jnp.int32)
    half = jax.ShapeDtypeStruct((DEPTH, 2048), jnp.bfloat16)

    mine = jnp.broadcast_to(amplitudes.reshape(1, 4, DEPTH), (16, 4, DEPTH))
    near = lax.all_to_all(mine, "z", 0, 0, tiled=True).reshape(GROUP, DEPTH)

    panel = integrals.reshape(3, LANES, 4, 4, LANES).transpose(0, 1, 3, 2, 4).reshape(DEPTH * 16, LANES)
    orbital = orbital_irrep.reshape(4, LANES)
    pair = pair_irrep.reshape(4, LANES)

    v_high, v_low = call(
        prepare_kernel,
        "prepare",
        3,
        [half, half],
        [place, slab_irrep, orbital_irrep, orbital, panel],
        [
            pltpu.VMEM((DEPTH * 16, LANES), jnp.float32),
            pltpu.VMEM((DEPTH, 2048), jnp.bfloat16),
            pltpu.VMEM((DEPTH, 2048), jnp.bfloat16),
            pltpu.SemaphoreType.DMA((9,)),
        ],
        cost=(8_000_000, 7_000_000),
        out_specs=[HBM, HBM],
        vmem=58,
        any_last=1,
    )

    def plan(turn):
        return call(
            plan_kernel,
            "plan",
            2,
            [i32((4, LANES)), i32((4, LANES)), i32((4, 2 * LANES)), i32((GROUP, LANES)), i32((1,)), i32((1,))],
            [turn.reshape(1), place, pair],
            [pltpu.VMEM((LANES, LANES), jnp.int32)],
            out_specs=[VMEM, VMEM, VMEM, VMEM, SMEM, SMEM],
        )

    def gather(sent, mates):
        packed = call(
            pack_kernel,
            "pack",
            2,
            f32((8 * KEPT, DEPTH)),
            [place, slab_irrep, orbital, mates, sent, near],
        )
        packed = packed.reshape(8, KEPT, DEPTH)
        return lax.all_to_all(packed, ("y", "xh"), 0, 0, tiled=True).reshape(8 * KEPT, DEPTH)

    def work(size, targets, gathered):
        keep, send = call(
            functools.partial(ladder_kernel, size),
            "ladder",
            2,
            [f32((32 * size, LANES))] * 2,
            [place, slab_irrep, orbital, targets, gathered, v_high, v_low],
            vmem=16,
        )
        arrived = lax.ppermute(send, "core", [(0, 1), (1, 0)])
        summed, other = call(
            functools.partial(add_kernel, size),
            "add",
            1,
            [f32((32 * size, LANES)), f32((16 * size, LANES))],
            [place, keep, arrived],
        )
        other = lax.ppermute(other, "xl", [(0, 1), (1, 0)])
        traded = lax.all_to_all(summed.reshape(16, 2 * size, LANES), ("y", "xh", "xl"), 0, 0, tiled=True)
        turned = call(
            functools.partial(turn_kernel, size),
            "turn",
            0,
            f32((16 * size, LANES)),
            [traded.reshape(32 * size, LANES)],
            [pltpu.VMEM((512, LANES), jnp.float32)],
        )
        tile = 4 if size % 8 else 8
        swapped = lax.all_to_all(turned.reshape(16, size // tile, tile, LANES), "z", 0, 0, tiled=True)
        swapped = swapped.reshape(16 * size, LANES)
        return (summed, other, swapped), (keep, arrived)

    def spread(size, out_shape, rounds, slots, found, held=()):
        return call(
            functools.partial(spread_kernel, size),
            "spread",
            5,
            out_shape,
            [place, rounds, slots, pair_irrep, orbital_irrep, orbital, *found, *held],
            [
                pltpu.VMEM((512, LANES), jnp.float32),
                pltpu.VMEM((16 * size, LANES), jnp.float32),
                pltpu.VMEM((2048, LANES), jnp.float32),
                pltpu.SemaphoreType.DMA((4,)),
            ],
            out_specs=jax.tree.map(lambda _: HBM, out_shape),
            any_last=len(held),
        )

    sent, slots, targets, mates, rounds, choice = plan(jnp.int32(0))
    near, v_high, v_low, sent, mates = lax.optimization_barrier((near, v_high, v_low, sent, mates))
    gathered = gather(sent, mates)

    def unpacked(filled):
        return filled.reshape(LANES, 4, 4, LANES).transpose(0, 2, 1, 3).reshape(LANES, 4, 512)

    def few(size, targets, gathered):
        found, _ = work(size, targets, gathered)
        return unpacked(spread(size, f32((2048, LANES)), rounds, slots, found))

    def many(targets, gathered):
        found, spare = work(SLOTS, targets, gathered)

        def later(state):
            turn, held = state
            sent, slots, targets, mates, _, _ = plan(turn)
            found, _ = work(SLOTS, targets, gather(sent, mates))
            return turn + 1, tuple(spread(SLOTS, [f32((1024, LANES))] * 2, rounds, slots, found, held))

        found, spare, turn = lax.optimization_barrier((found, spare, jnp.int32(1)))
        _, held = lax.while_loop(lambda state: state[0] < rounds[0], later, (turn, spare))
        return unpacked(spread(SLOTS, f32((2048, LANES)), rounds, slots, found, held))

    ways = [functools.partial(few, size) for size in FEWER] + [many]
    return lax.switch(choice[0], ways, targets, gathered)


def solution(mesh):
    devices = np.asarray(mesh.devices).reshape(4, 2, 16, 2, 2)
    fine = Mesh(devices, ("y", "xh", "z", "xl", "core"))
    blocks, groups = ("y", "xh", "z"), ("xl", "core")
    placed = (P(blocks, None, groups), P(None, groups, blocks, None), P(), P(), P())
    return jax.shard_map(
        on_device,
        mesh=fine,
        in_specs=placed,
        out_specs=P(groups, blocks, None),
        check_vma=False,
    )
```

```python
import functools

import jax
import jax.numpy as jnp
import numpy as np
from jax import lax
from jax.experimental import pallas as pl
from jax.experimental.pallas import tpu as pltpu
from jax.sharding import Mesh
from jax.sharding import PartitionSpec as P

LANES = 128
GROUP = 64
SLOTS = 32
FEWER = (24, 28)
KEPT = 24
HALF = 16
DEPTH = 3 * LANES
VMEM = pl.BlockSpec(memory_space=pltpu.VMEM)
SMEM = pl.BlockSpec(memory_space=pltpu.SMEM)
HBM = pl.BlockSpec(memory_space=pltpu.HBM)


def split(x):
    high = x.astype(jnp.bfloat16)
    return high, (x - high.astype(jnp.float32)).astype(jnp.bfloat16)


def dot(x, y):
    return jnp.dot(x, y, preferred_element_type=jnp.float32)


def iota(shape, dim):
    return lax.broadcasted_iota(jnp.int32, shape, dim)


def count(where):
    return jnp.sum(jnp.where(where, 1, 0), axis=0, keepdims=True)


def column_of(row):
    return jnp.transpose(jnp.broadcast_to(row, (LANES, LANES)))


def plan_kernel(turn, place, pair, sent, slots, targets, mates, rounds, choice, column_s):
    source, lane = iota((LANES, LANES), 0), iota((LANES, LANES), 1)
    near = source < GROUP
    mate = near == (lane < GROUP)
    later = iota((1, LANES), 1) >= GROUP
    ranks, firsts, starts = [], [], []
    most, total = 0, 0
    for q in range(4):
        row = pair[q : q + 1, :]
        column = column_of(row)
        same = column == row

        ranks.append(count(same & mate & (source < lane)))
        firsts.append(count(same & near))
        most = jnp.maximum(most, jnp.max(count(same & mate)))
        total = jnp.maximum(total, jnp.max(count(same)))
        starts.append([count((column == (lane + t * LANES) // KEPT) & near) for t in range(2)])
    one = (most <= KEPT) & (total <= SLOTS)
    rounds[0] = jnp.where(one, 1, (most + HALF - 1) // HALF)
    fewer = jnp.where(total <= FEWER[0], 0, jnp.where(total <= FEWER[1], 1, 2))
    choice[0] = jnp.where(one, fewer, 2)
    shift = turn[0] * HALF
    for q in range(4):
        window = ranks[q] - shift
        window = jnp.where((window >= 0) & (window < HALF), window, -1)
        chosen = jnp.where(one, ranks[q], window)
        base = jnp.where(one, firsts[q], HALF)
        sent[q : q + 1, :] = chosen
        slots[q : q + 1, :] = jnp.where(chosen < 0, -1, chosen + jnp.where(later, base, 0))
        for t in range(2):
            spot = (iota((1, LANES), 1) + t * LANES) % KEPT
            start = jnp.where(one, starts[q][t], HALF)
            targets[q : q + 1, t * LANES : (t + 1) * LANES] = spot + start
    column_s[...] = column_of(pair[pl.ds(place[5], 1), :])
    mates[...] = column_s[pl.ds(pl.multiple_of(place[6] * GROUP, GROUP), GROUP), :]


def pack_kernel(place, slab, orbital, mates, sent, near, out):
    occ, quarter, later = place[1], place[5], place[6]
    depth_row = orbital[pl.ds(occ, 1), :]
    column = mates[...]
    chosen = sent[pl.ds(quarter, 1), :]
    chosen = jnp.where(later == 1, pltpu.roll(chosen, GROUP, 1), chosen)[:, :GROUP]
    pick = jnp.where(iota((KEPT, GROUP), 0) == chosen, 1.0, 0.0).astype(jnp.bfloat16)
    for c in range(3):
        lanes = slice(c * LANES, (c + 1) * LANES)
        high, low = split(jnp.where(column == depth_row ^ slab[c], near[:, lanes], 0.0))
        kept = dot(pick, high) + dot(pick, low)
        for to in range(8):
            out[to * KEPT : (to + 1) * KEPT, lanes] = kept


def prepare_kernel(place, slab, orbital_s, orbital, integrals, v_high, v_low, panels, high, low, done):
    block, occ = place[0], place[1]
    depth_row = orbital[pl.ds(occ, 1), :]

    def part_of(c):
        rows = pl.ds(c * LANES * 16, LANES * 16)
        return pltpu.make_async_copy(integrals.at[rows, :], panels.at[rows, :], done.at[c])

    def results_of(c):
        rows = pl.ds(c * LANES, LANES)
        yield pltpu.make_async_copy(high.at[rows, :], v_high.at[rows, :], done.at[3 + 2 * c])
        yield pltpu.make_async_copy(low.at[rows, :], v_low.at[rows, :], done.at[4 + 2 * c])

    for c in range(3):
        part_of(c).start()
    for c in range(3):
        depth = column_of(depth_row ^ slab[c])
        part_of(c).wait()
        for y in range(4):
            lanes = orbital[y : y + 1, :]
            for i in range(4):
                panel = panels[pl.ds(c * LANES * 16 + y * 4 + i, LANES, stride=16), :]
                label = lanes ^ orbital_s[block * 4 + i]
                parts = split(jnp.where(depth == label, panel, 0.0))
                columns = slice((y * 4 + i) * LANES, (y * 4 + i + 1) * LANES)
                high[c * LANES : (c + 1) * LANES, columns], low[c * LANES : (c + 1) * LANES, columns] = parts
        for copy in results_of(c):
            copy.start()
    for c in range(3):
        for copy in results_of(c):
            copy.wait()


def ladder_kernel(size, place, slab, orbital, targets, gathered, v_high, v_low, keep, send):
    occ, core = place[1], place[2]
    depth_row = orbital[pl.ds(occ, 1), :]
    depth_row = jnp.concatenate([depth_row ^ slab[c] for c in range(3)], axis=1)
    width = -(-size // 8) * 8
    slot = iota((width, 8 * KEPT), 0)
    highs, lows = [], []
    for half in range(2):
        for x in range(2):
            quarter = 2 * x + (core ^ half)
            pick = jnp.where(slot == targets[pl.ds(quarter, 1), : 8 * KEPT], 1.0, 0.0).astype(jnp.bfloat16)
            first = gathered[pl.ds(pl.multiple_of(quarter * 2 * KEPT, 8), KEPT), :]
            second = gathered[pl.ds(pl.multiple_of(quarter * 2 * KEPT + KEPT, 8), KEPT), :]
            second = jnp.concatenate([jnp.where(depth_row == l, second, 0.0) for l in range(8)], axis=0)
            if width > KEPT:
                first = jnp.concatenate([first, jnp.zeros((width - KEPT, DEPTH), jnp.float32)], axis=0)
            for to, one, two in zip((highs, lows), split(first), split(second)):
                to.append(one.astype(jnp.float32) + dot(pick, two))
    rows = 4 * width
    t_both = jnp.concatenate(highs + lows, axis=0).astype(jnp.bfloat16)
    t_high = jnp.concatenate(highs, axis=0).astype(jnp.bfloat16)
    near = iota((rows, LANES), 1) < 64
    for y in range(4):
        panel = slice(y * 512, (y + 1) * 512)
        parts = dot(t_both, v_high[:, panel])
        total = parts[:rows] + parts[rows:] + dot(t_high, v_low[:, panel])
        for m in range(2):
            even, odd = total[:, 2 * m * LANES : (2 * m + 1) * LANES], total[:, (2 * m + 1) * LANES : (2 * m + 2) * LANES]
            cut = (
                jnp.where(near, even, pltpu.roll(odd, 64, 1)),
                jnp.where(near, pltpu.roll(even, 64, 1), odd),
            )
            for half, out in ((0, keep), (1, send)):
                for x in range(2):
                    at = (half * 2 + x) * width
                    for h in range(2):
                        to = (((y * 2 + h) * 2 + x) * 2 + m) * size
                        out[to : to + size, :] = cut[h][at : at + size]


def add_kernel(size, place, keep, arrived, summed, other):
    x = place[4]
    summed[...] = keep[...] + arrived[...]
    for block in range(8):
        rows = pl.ds(pl.multiple_of((block * 2 + 1 - x) * 2 * size, 8), 2 * size)
        other[block * 2 * size : (block + 1) * 2 * size, :] = summed[rows, :]


def folded(size):
    spare, gap = LANES - 4 * size, SLOTS - size
    for t in range(gap):
        yield size + t, [(u * gap + t, spare * u) for u in range(size // gap)]


def turn_kernel(size, arrived, out, turned):
    lane = iota((16, LANES), 1)
    for h in range(2):
        for m in range(2):
            rows = []
            for y in range(4):
                at = (y * 2 + h) * 4 * size + m * size
                rows.append(arrived[at : at + size, :] + arrived[2 * size + at : 2 * size + at + size, :])
            if size < SLOTS:
                rows.append(jnp.zeros((LANES - 4 * size, LANES), jnp.float32))
            at = (h * 2 + m) * LANES
            turned[at : at + LANES, :] = jnp.transpose(jnp.concatenate(rows, axis=0))

    def part(row):
        j, h, i = row // 8, row // 4 % 2, row % 4
        return turned[pl.ds((h * 2 + i // 2) * LANES + i % 2 * 64 + j, 16, stride=4), :]

    if size == SLOTS:
        for row in range(size):
            out[pl.ds(row, 16, stride=size), :] = part(row)
    for last, pieces in folded(size):
        spread_out = part(last)
        for row, at in pieces:
            out[pl.ds(row, 16, stride=size), :] = jnp.where(
                lane < 4 * size, part(row), pltpu.roll(spread_out, 4 * size - at, 1)
            )


def spread_kernel(size, place, rounds, slots, labels, orbital_s, orbital, summed, other, swapped, *rest):
    *rest, turned, packed, filled, done = rest
    held, outs = (rest[:2], rest[2:]) if size == SLOTS else ((), rest)
    block, occ, x = place[0], place[1], place[4]
    lane = iota((16, LANES), 1)

    def put(row, part):
        j, h, i = row // 8, row // 4 % 2, row % 4
        turned[pl.ds(j * LANES + h * 64 + i, 16, stride=4), :] = part

    if size == SLOTS:
        for row in range(size):
            put(row, swapped[pl.ds(row, 16, stride=size), :])
    for last, pieces in folded(size):
        whole = None
        for row, at in pieces:
            part = swapped[pl.ds(row, 16, stride=size), :]
            put(row, part)
            piece = pltpu.roll(part, (at - 4 * size) % LANES, 1)
            whole = piece if whole is None else jnp.where(lane < at, whole, piece)
        put(last, whole)
    mirrored = [jnp.transpose(turned[j * LANES : (j + 1) * LANES, :]) for j in range(4)]
    near = iota((size, LANES), 1) < 64
    for y in range(4):
        for m in range(2):
            cut = []
            for h in range(2):
                at = (y * 2 + h) * 2 * size + m * size
                mine = summed[pl.ds(pl.multiple_of(((y * 2 + h) * 2 + x) * 2 * size, 8), 2 * size), :]
                cut.append(mine[m * size : (m + 1) * size] + other[at : at + size, :])
            own = (
                jnp.where(near, cut[0], pltpu.roll(cut[1], 64, 1)),
                jnp.where(near, pltpu.roll(cut[0], 64, 1), cut[1]),
            )
            for e in range(2):
                j = 2 * m + e
                packed[pl.ds(y * 4 + j, size, stride=16), :] = own[e] - mirrored[j][y * size : (y + 1) * size]
    rows = []
    for y in range(4):
        for j in range(4):
            rows.append(orbital[y : y + 1, :] ^ orbital_s[block * 4 + j])
    entry = jnp.concatenate(rows, axis=0)

    def rows_of(p):
        return pl.ds(pl.multiple_of(p * 16, 16), 16)

    def store(p):
        values = packed[pl.ds(pl.multiple_of(slots[occ, p] * 16, 16), 16), :]
        filled[rows_of(p), :] = jnp.where(entry == labels[occ * LANES + p], values, 0.0)

    def part_of(part):
        share = 4 // len(outs)
        to = outs[part // share].at[pl.ds(part % share * 512, 512), :]
        return pltpu.make_async_copy(filled.at[pl.ds(part * 512, 512), :], to, done.at[part])

    def fill():
        def step(p, carry):
            store(p)
            return carry

        for part in range(4):
            lax.fori_loop(part * 32, part * 32 + 32, step, 0, unroll=8)
            part_of(part).start()

    def fill_in():
        for half in range(2):
            copy = pltpu.make_async_copy(held[half], filled.at[pl.ds(half * 1024, 1024), :], done.at[half])
            copy.start()
            copy.wait()

        def step(p, carry):
            pl.when(slots[occ, p] >= 0)(lambda: store(p))
            return carry

        lax.fori_loop(0, LANES, step, 0)
        for part in range(4):
            part_of(part).start()

    if held:
        pl.when(rounds[0] > 1)(fill_in)
        pl.when(rounds[0] <= 1)(fill)
    else:
        fill()
    for part in range(4):
        part_of(part).wait()


def call(kernel, name, scalars, out_shape, operands, scratch=(), cost=None, out_specs=None, vmem=8, any_last=0):
    return pl.pallas_call(
        kernel,
        out_shape=out_shape,
        in_specs=[SMEM] * scalars + [VMEM] * (len(operands) - scalars - any_last) + [HBM] * any_last,
        out_specs=out_specs or jax.tree.map(lambda _: VMEM, out_shape),
        scratch_shapes=list(scratch),
        compiler_params=pltpu.CompilerParams(vmem_limit_bytes=vmem * 1024 * 1024),
        cost_estimate=cost and pl.CostEstimate(flops=cost[0], bytes_accessed=cost[1], transcendentals=0),
        name=name,
    )(*operands)


def on_device(amplitudes, integrals, orbital_irrep, slab_irrep, pair_irrep):
    y, xh, z = lax.axis_index("y"), lax.axis_index("xh"), lax.axis_index("z")
    x, core = lax.axis_index("xl"), lax.axis_index("core")
    block, occ = (y * 2 + xh) * 16 + z, x * 2 + core
    place = jnp.stack([block, occ, core, 0, x, y, xh]).astype(jnp.int32)
    f32 = functools.partial(jax.ShapeDtypeStruct, dtype=jnp.float32)
    i32 = functools.partial(jax.ShapeDtypeStruct, dtype=jnp.int32)
    half = jax.ShapeDtypeStruct((DEPTH, 2048), jnp.bfloat16)

    mine = jnp.broadcast_to(amplitudes.reshape(1, 4, DEPTH), (16, 4, DEPTH))
    near = lax.all_to_all(mine, "z", 0, 0, tiled=True).reshape(GROUP, DEPTH)

    panel = integrals.reshape(3, LANES, 4, 4, LANES).transpose(0, 1, 3, 2, 4).reshape(DEPTH * 16, LANES)
    orbital = orbital_irrep.reshape(4, LANES)
    pair = pair_irrep.reshape(4, LANES)

    v_high, v_low = call(
        prepare_kernel,
        "prepare",
        3,
        [half, half],
        [place, slab_irrep, orbital_irrep, orbital, panel],
        [
            pltpu.VMEM((DEPTH * 16, LANES), jnp.float32),
            pltpu.VMEM((DEPTH, 2048), jnp.bfloat16),
            pltpu.VMEM((DEPTH, 2048), jnp.bfloat16),
            pltpu.SemaphoreType.DMA((9,)),
        ],
        cost=(8_000_000, 7_000_000),
        out_specs=[HBM, HBM],
        vmem=58,
        any_last=1,
    )

    def plan(turn):
        return call(
            plan_kernel,
            "plan",
            2,
            [i32((4, LANES)), i32((4, LANES)), i32((4, 2 * LANES)), i32((GROUP, LANES)), i32((1,)), i32((1,))],
            [turn.reshape(1), place, pair],
            [pltpu.VMEM((LANES, LANES), jnp.int32)],
            out_specs=[VMEM, VMEM, VMEM, VMEM, SMEM, SMEM],
        )

    def gather(sent, mates):
        packed = call(
            pack_kernel,
            "pack",
            2,
            f32((8 * KEPT, DEPTH)),
            [place, slab_irrep, orbital, mates, sent, near],
        )
        packed = packed.reshape(8, KEPT, DEPTH)
        return lax.all_to_all(packed, ("y", "xh"), 0, 0, tiled=True).reshape(8 * KEPT, DEPTH)

    def work(size, targets, gathered):
        keep, send = call(
            functools.partial(ladder_kernel, size),
            "ladder",
            2,
            [f32((32 * size, LANES))] * 2,
            [place, slab_irrep, orbital, targets, gathered, v_high, v_low],
            vmem=16,
        )
        arrived = lax.ppermute(send, "core", [(0, 1), (1, 0)])
        summed, other = call(
            functools.partial(add_kernel, size),
            "add",
            1,
            [f32((32 * size, LANES)), f32((16 * size, LANES))],
            [place, keep, arrived],
        )
        other = lax.ppermute(other, "xl", [(0, 1), (1, 0)])
        traded = lax.all_to_all(summed.reshape(16, 2 * size, LANES), ("y", "xh", "xl"), 0, 0, tiled=True)
        turned = call(
            functools.partial(turn_kernel, size),
            "turn",
            0,
            f32((16 * size, LANES)),
            [traded.reshape(32 * size, LANES)],
            [pltpu.VMEM((512, LANES), jnp.float32)],
        )
        tile = 4 if size % 8 else 8
        swapped = lax.all_to_all(turned.reshape(16, size // tile, tile, LANES), "z", 0, 0, tiled=True)
        swapped = swapped.reshape(16 * size, LANES)
        return (summed, other, swapped), (keep, arrived)

    def spread(size, out_shape, rounds, slots, found, held=()):
        return call(
            functools.partial(spread_kernel, size),
            "spread",
            5,
            out_shape,
            [place, rounds, slots, pair_irrep, orbital_irrep, orbital, *found, *held],
            [
                pltpu.VMEM((512, LANES), jnp.float32),
                pltpu.VMEM((16 * size, LANES), jnp.float32),
                pltpu.VMEM((2048, LANES), jnp.float32),
                pltpu.SemaphoreType.DMA((4,)),
            ],
            out_specs=jax.tree.map(lambda _: HBM, out_shape),
            any_last=len(held),
        )

    sent, slots, targets, mates, rounds, choice = plan(jnp.int32(0))
    near, v_high, v_low, sent, mates = lax.optimization_barrier((near, v_high, v_low, sent, mates))
    gathered = gather(sent, mates)

    def unpacked(filled):
        return filled.reshape(LANES, 4, 4, LANES).transpose(0, 2, 1, 3).reshape(LANES, 4, 512)

    def few(size, targets, gathered):
        found, _ = work(size, targets, gathered)
        return unpacked(spread(size, f32((2048, LANES)), rounds, slots, found))

    def many(targets, gathered):
        found, spare = work(SLOTS, targets, gathered)

        def later(state):
            turn, held = state
            sent, slots, targets, mates, _, _ = plan(turn)
            found, _ = work(SLOTS, targets, gather(sent, mates))
            return turn + 1, tuple(spread(SLOTS, [f32((1024, LANES))] * 2, rounds, slots, found, held))

        found, spare, turn = lax.optimization_barrier((found, spare, jnp.int32(1)))
        _, held = lax.while_loop(lambda state: state[0] < rounds[0], later, (turn, spare))
        return unpacked(spread(SLOTS, f32((2048, LANES)), rounds, slots, found, held))

    ways = [functools.partial(few, size) for size in FEWER] + [many]
    return lax.switch(choice[0], ways, targets, gathered)


def solution(mesh):
    devices = np.asarray(mesh.devices).reshape(4, 2, 16, 2, 2)
    fine = Mesh(devices, ("y", "xh", "z", "xl", "core"))
    blocks, groups = ("y", "xh", "z"), ("xl", "core")
    placed = (P(blocks, None, groups), P(None, groups, blocks, None), P(), P(), P())
    return jax.shard_map(
        on_device,
        mesh=fine,
        in_specs=placed,
        out_specs=P(groups, blocks, None),
        check_vma=False,
    )
```

```python
import functools

import jax
import jax.numpy as jnp
import numpy as np
from jax import lax
from jax.experimental import pallas as pl
from jax.experimental.pallas import tpu as pltpu
from jax.sharding import Mesh
from jax.sharding import PartitionSpec as P

LANES = 128
GROUP = 64
SLOTS = 32
FEWER = (24, 28)
KEPT = 24
HALF = 16
DEPTH = 3 * LANES
VMEM = pl.BlockSpec(memory_space=pltpu.VMEM)
SMEM = pl.BlockSpec(memory_space=pltpu.SMEM)
HBM = pl.BlockSpec(memory_space=pltpu.HBM)


def split(x):
    high = x.astype(jnp.bfloat16)
    return high, (x - high.astype(jnp.float32)).astype(jnp.bfloat16)


def dot(x, y):
    return jnp.dot(x, y, preferred_element_type=jnp.float32)


def iota(shape, dim):
    return lax.broadcasted_iota(jnp.int32, shape, dim)


def count(where):
    return jnp.sum(jnp.where(where, 1, 0), axis=0, keepdims=True)


def column_of(row):
    return jnp.transpose(jnp.broadcast_to(row, (LANES, LANES)))


def plan_kernel(turn, place, pair, sent, slots, targets, mates, rounds, choice, column_s):
    source, lane = iota((LANES, LANES), 0), iota((LANES, LANES), 1)
    near = source < GROUP
    mate = near == (lane < GROUP)
    later = iota((1, LANES), 1) >= GROUP
    ranks, firsts, starts = [], [], []
    most, total = 0, 0
    for q in range(4):
        row = pair[q : q + 1, :]
        column = column_of(row)
        same = column == row

        ranks.append(count(same & mate & (source < lane)))
        firsts.append(count(same & near))
        most = jnp.maximum(most, jnp.max(count(same & mate)))
        total = jnp.maximum(total, jnp.max(count(same)))
        starts.append([count((column == (lane + t * LANES) // KEPT) & near) for t in range(2)])
    one = (most <= KEPT) & (total <= SLOTS)
    rounds[0] = jnp.where(one, 1, (most + HALF - 1) // HALF)
    fewer = jnp.where(total <= FEWER[0], 0, jnp.where(total <= FEWER[1], 1, 2))
    choice[0] = jnp.where(one, fewer, 2)
    shift = turn[0] * HALF
    for q in range(4):
        window = ranks[q] - shift
        window = jnp.where((window >= 0) & (window < HALF), window, -1)
        chosen = jnp.where(one, ranks[q], window)
        base = jnp.where(one, firsts[q], HALF)
        sent[q : q + 1, :] = chosen
        slots[q : q + 1, :] = jnp.where(chosen < 0, -1, chosen + jnp.where(later, base, 0))
        for t in range(2):
            spot = (iota((1, LANES), 1) + t * LANES) % KEPT
            start = jnp.where(one, starts[q][t], HALF)
            targets[q : q + 1, t * LANES : (t + 1) * LANES] = spot + start
    column_s[...] = column_of(pair[pl.ds(place[5], 1), :])
    mates[...] = column_s[pl.ds(pl.multiple_of(place[6] * GROUP, GROUP), GROUP), :]


def pack_kernel(place, slab, orbital, mates, sent, near, out):
    occ, quarter, later = place[1], place[5], place[6]
    depth_row = orbital[pl.ds(occ, 1), :]
    column = mates[...]
    chosen = sent[pl.ds(quarter, 1), :]
    chosen = jnp.where(later == 1, pltpu.roll(chosen, GROUP, 1), chosen)[:, :GROUP]
    pick = jnp.where(iota((KEPT, GROUP), 0) == chosen, 1.0, 0.0).astype(jnp.bfloat16)
    for c in range(3):
        lanes = slice(c * LANES, (c + 1) * LANES)
        high, low = split(jnp.where(column == depth_row ^ slab[c], near[:, lanes], 0.0))
        kept = dot(pick, high) + dot(pick, low)
        for to in range(8):
            out[to * KEPT : (to + 1) * KEPT, lanes] = kept


def prepare_kernel(place, slab, orbital_s, orbital, integrals, v_high, v_low, panels, high, low, done):
    block, occ = place[0], place[1]
    depth_row = orbital[pl.ds(occ, 1), :]

    def part_of(c):
        rows = pl.ds(c * LANES * 16, LANES * 16)
        return pltpu.make_async_copy(integrals.at[rows, :], panels.at[rows, :], done.at[c])

    def results_of(c):
        rows = pl.ds(c * LANES, LANES)
        yield pltpu.make_async_copy(high.at[rows, :], v_high.at[rows, :], done.at[3 + 2 * c])
        yield pltpu.make_async_copy(low.at[rows, :], v_low.at[rows, :], done.at[4 + 2 * c])

    for c in range(3):
        part_of(c).start()
    for c in range(3):
        depth = column_of(depth_row ^ slab[c])
        part_of(c).wait()
        for y in range(4):
            lanes = orbital[y : y + 1, :]
            for i in range(4):
                panel = panels[pl.ds(c * LANES * 16 + y * 4 + i, LANES, stride=16), :]
                label = lanes ^ orbital_s[block * 4 + i]
                parts = split(jnp.where(depth == label, panel, 0.0))
                columns = slice((y * 4 + i) * LANES, (y * 4 + i + 1) * LANES)
                high[c * LANES : (c + 1) * LANES, columns], low[c * LANES : (c + 1) * LANES, columns] = parts
        for copy in results_of(c):
            copy.start()
    for c in range(3):
        for copy in results_of(c):
            copy.wait()


def ladder_kernel(size, place, slab, orbital, targets, gathered, v_high, v_low, keep, send):
    occ, core = place[1], place[2]
    depth_row = orbital[pl.ds(occ, 1), :]
    depth_row = jnp.concatenate([depth_row ^ slab[c] for c in range(3)], axis=1)
    width = -(-size // 8) * 8
    slot = iota((width, 8 * KEPT), 0)
    highs, lows = [], []
    for half in range(2):
        for x in range(2):
            quarter = 2 * x + (core ^ half)
            pick = jnp.where(slot == targets[pl.ds(quarter, 1), : 8 * KEPT], 1.0, 0.0).astype(jnp.bfloat16)
            first = gathered[pl.ds(pl.multiple_of(quarter * KEPT, 8), KEPT), :]
            second = gathered[pl.ds(pl.multiple_of((4 + quarter) * KEPT, 8), KEPT), :]
            second = jnp.concatenate([jnp.where(depth_row == l, second, 0.0) for l in range(8)], axis=0)
            if width > KEPT:
                first = jnp.concatenate([first, jnp.zeros((width - KEPT, DEPTH), jnp.float32)], axis=0)
            for to, one, two in zip((highs, lows), split(first), split(second)):
                to.append(one.astype(jnp.float32) + dot(pick, two))
    rows = 4 * width
    t_both = jnp.concatenate(highs + lows, axis=0).astype(jnp.bfloat16)
    t_high = jnp.concatenate(highs, axis=0).astype(jnp.bfloat16)
    near = iota((rows, LANES), 1) < 64
    for y in range(4):
        panel = slice(y * 512, (y + 1) * 512)
        parts = dot(t_both, v_high[:, panel])
        total = parts[:rows] + parts[rows:] + dot(t_high, v_low[:, panel])
        for m in range(2):
            even, odd = total[:, 2 * m * LANES : (2 * m + 1) * LANES], total[:, (2 * m + 1) * LANES : (2 * m + 2) * LANES]
            cut = (
                jnp.where(near, even, pltpu.roll(odd, 64, 1)),
                jnp.where(near, pltpu.roll(even, 64, 1), odd),
            )
            for half, out in ((0, keep), (1, send)):
                for x in range(2):
                    at = (half * 2 + x) * width
                    for h in range(2):
                        to = (((h * 2 + x) * 4 + y) * 2 + m) * size
                        out[to : to + size, :] = cut[h][at : at + size]


def add_kernel(size, place, keep, arrived, summed, other):
    x = place[4]
    summed[...] = keep[...] + arrived[...]
    for h in range(2):
        rows = pl.ds(pl.multiple_of((h * 2 + 1 - x) * 8 * size, 8), 8 * size)
        other[h * 8 * size : (h + 1) * 8 * size, :] = summed[rows, :]


def folded(size):
    spare, gap = LANES - 4 * size, SLOTS - size
    for t in range(gap):
        yield size + t, [(u * gap + t, spare * u) for u in range(size // gap)]


def turn_kernel(size, arrived, out, turned):
    lane = iota((16, LANES), 1)
    for h in range(2):
        for m in range(2):
            rows = []
            for y in range(4):
                at = (h * 8 + y) * 2 * size + m * size
                rows.append(arrived[at : at + size, :] + arrived[8 * size + at : 8 * size + at + size, :])
            if size < SLOTS:
                rows.append(jnp.zeros((LANES - 4 * size, LANES), jnp.float32))
            at = (h * 2 + m) * LANES
            turned[at : at + LANES, :] = jnp.transpose(jnp.concatenate(rows, axis=0))

    def part(row):
        j, h, i = row // 8, row // 4 % 2, row % 4
        return turned[pl.ds((h * 2 + i // 2) * LANES + i % 2 * 64 + j, 16, stride=4), :]

    if size == SLOTS:
        for row in range(size):
            out[pl.ds(row, 16, stride=size), :] = part(row)
    for last, pieces in folded(size):
        spread_out = part(last)
        for row, at in pieces:
            out[pl.ds(row, 16, stride=size), :] = jnp.where(
                lane < 4 * size, part(row), pltpu.roll(spread_out, 4 * size - at, 1)
            )


def spread_kernel(size, place, rounds, slots, labels, orbital_s, orbital, summed, other, swapped, *rest):
    *rest, turned, packed, filled, done = rest
    held, outs = (rest[:2], rest[2:]) if size == SLOTS else ((), rest)
    block, occ, x = place[0], place[1], place[4]
    lane = iota((16, LANES), 1)

    def put(row, part):
        j, h, i = row // 8, row // 4 % 2, row % 4
        turned[pl.ds(j * LANES + h * 64 + i, 16, stride=4), :] = part

    if size == SLOTS:
        for row in range(size):
            put(row, swapped[pl.ds(row, 16, stride=size), :])
    for last, pieces in folded(size):
        whole = None
        for row, at in pieces:
            part = swapped[pl.ds(row, 16, stride=size), :]
            put(row, part)
            piece = pltpu.roll(part, (at - 4 * size) % LANES, 1)
            whole = piece if whole is None else jnp.where(lane < at, whole, piece)
        put(last, whole)
    mirrored = [jnp.transpose(turned[j * LANES : (j + 1) * LANES, :]) for j in range(4)]
    near = iota((size, LANES), 1) < 64
    for y in range(4):
        for m in range(2):
            cut = []
            for h in range(2):
                at = (h * 4 + y) * 2 * size + m * size
                mine = summed[pl.ds(pl.multiple_of(((h * 2 + x) * 4 + y) * 2 * size, 8), 2 * size), :]
                cut.append(mine[m * size : (m + 1) * size] + other[at : at + size, :])
            own = (
                jnp.where(near, cut[0], pltpu.roll(cut[1], 64, 1)),
                jnp.where(near, pltpu.roll(cut[0], 64, 1), cut[1]),
            )
            for e in range(2):
                j = 2 * m + e
                packed[pl.ds(y * 4 + j, size, stride=16), :] = own[e] - mirrored[j][y * size : (y + 1) * size]
    rows = []
    for y in range(4):
        for j in range(4):
            rows.append(orbital[y : y + 1, :] ^ orbital_s[block * 4 + j])
    entry = jnp.concatenate(rows, axis=0)

    def rows_of(p):
        return pl.ds(pl.multiple_of(p * 16, 16), 16)

    def store(p):
        values = packed[pl.ds(pl.multiple_of(slots[occ, p] * 16, 16), 16), :]
        filled[rows_of(p), :] = jnp.where(entry == labels[occ * LANES + p], values, 0.0)

    def part_of(part):
        share = 4 // len(outs)
        to = outs[part // share].at[pl.ds(part % share * 512, 512), :]
        return pltpu.make_async_copy(filled.at[pl.ds(part * 512, 512), :], to, done.at[part])

    def fill():
        def step(p, carry):
            store(p)
            return carry

        for part in range(4):
            lax.fori_loop(part * 32, part * 32 + 32, step, 0, unroll=32)
            part_of(part).start()

    def fill_in():
        for half in range(2):
            copy = pltpu.make_async_copy(held[half], filled.at[pl.ds(half * 1024, 1024), :], done.at[half])
            copy.start()
            copy.wait()

        def step(p, carry):
            pl.when(slots[occ, p] >= 0)(lambda: store(p))
            return carry

        lax.fori_loop(0, LANES, step, 0)
        for part in range(4):
            part_of(part).start()

    if held:
        pl.when(rounds[0] > 1)(fill_in)
        pl.when(rounds[0] <= 1)(fill)
    else:
        fill()
    for part in range(4):
        part_of(part).wait()


def call(kernel, name, scalars, out_shape, operands, scratch=(), cost=None, out_specs=None, vmem=8, any_last=0):
    return pl.pallas_call(
        kernel,
        out_shape=out_shape,
        in_specs=[SMEM] * scalars + [VMEM] * (len(operands) - scalars - any_last) + [HBM] * any_last,
        out_specs=out_specs or jax.tree.map(lambda _: VMEM, out_shape),
        scratch_shapes=list(scratch),
        compiler_params=pltpu.CompilerParams(vmem_limit_bytes=vmem * 1024 * 1024),
        cost_estimate=cost and pl.CostEstimate(flops=cost[0], bytes_accessed=cost[1], transcendentals=0),
        name=name,
    )(*operands)


def on_device(amplitudes, integrals, orbital_irrep, slab_irrep, pair_irrep):
    y, xh, z = lax.axis_index("y"), lax.axis_index("xh"), lax.axis_index("z")
    x, core = lax.axis_index("xl"), lax.axis_index("core")
    block, occ = (y * 2 + xh) * 16 + z, x * 2 + core
    place = jnp.stack([block, occ, core, 0, x, y, xh]).astype(jnp.int32)
    f32 = functools.partial(jax.ShapeDtypeStruct, dtype=jnp.float32)
    i32 = functools.partial(jax.ShapeDtypeStruct, dtype=jnp.int32)
    half = jax.ShapeDtypeStruct((DEPTH, 2048), jnp.bfloat16)

    mine = jnp.broadcast_to(amplitudes.reshape(1, 4, DEPTH), (16, 4, DEPTH))
    near = lax.all_to_all(mine, "z", 0, 0, tiled=True).reshape(GROUP, DEPTH)

    panel = integrals.reshape(3, LANES, 4, 4, LANES).transpose(0, 1, 3, 2, 4).reshape(DEPTH * 16, LANES)
    orbital = orbital_irrep.reshape(4, LANES)
    pair = pair_irrep.reshape(4, LANES)

    v_high, v_low = call(
        prepare_kernel,
        "prepare",
        3,
        [half, half],
        [place, slab_irrep, orbital_irrep, orbital, panel],
        [
            pltpu.VMEM((DEPTH * 16, LANES), jnp.float32),
            pltpu.VMEM((DEPTH, 2048), jnp.bfloat16),
            pltpu.VMEM((DEPTH, 2048), jnp.bfloat16),
            pltpu.SemaphoreType.DMA((9,)),
        ],
        cost=(8_000_000, 7_000_000),
        out_specs=[HBM, HBM],
        vmem=58,
        any_last=1,
    )

    def plan(turn):
        return call(
            plan_kernel,
            "plan",
            2,
            [i32((4, LANES)), i32((4, LANES)), i32((4, 2 * LANES)), i32((GROUP, LANES)), i32((1,)), i32((1,))],
            [turn.reshape(1), place, pair],
            [pltpu.VMEM((LANES, LANES), jnp.int32)],
            out_specs=[VMEM, VMEM, VMEM, VMEM, SMEM, SMEM],
        )

    def gather(sent, mates):
        packed = call(
            pack_kernel,
            "pack",
            2,
            f32((8 * KEPT, DEPTH)),
            [place, slab_irrep, orbital, mates, sent, near],
        )
        packed = packed.reshape(8, KEPT, DEPTH)
        return lax.all_to_all(packed, ("xh", "y"), 0, 0, tiled=True).reshape(8 * KEPT, DEPTH)

    def work(size, targets, gathered):
        keep, send = call(
            functools.partial(ladder_kernel, size),
            "ladder",
            2,
            [f32((32 * size, LANES))] * 2,
            [place, slab_irrep, orbital, targets, gathered, v_high, v_low],
            vmem=16,
        )
        arrived = lax.ppermute(send, "core", [(0, 1), (1, 0)])
        summed, other = call(
            functools.partial(add_kernel, size),
            "add",
            1,
            [f32((32 * size, LANES)), f32((16 * size, LANES))],
            [place, keep, arrived],
        )
        other = lax.ppermute(other, "xl", [(0, 1), (1, 0)])
        traded = lax.all_to_all(summed.reshape(16, 2 * size, LANES), ("xh", "xl", "y"), 0, 0, tiled=True)
        turned = call(
            functools.partial(turn_kernel, size),
            "turn",
            0,
            f32((16 * size, LANES)),
            [traded.reshape(32 * size, LANES)],
            [pltpu.VMEM((512, LANES), jnp.float32)],
        )
        tile = 4 if size % 8 else 8
        swapped = lax.all_to_all(turned.reshape(16, size // tile, tile, LANES), "z", 0, 0, tiled=True)
        swapped = swapped.reshape(16 * size, LANES)
        return (summed, other, swapped), (keep, arrived)

    def spread(size, out_shape, rounds, slots, found, held=()):
        return call(
            functools.partial(spread_kernel, size),
            "spread",
            5,
            out_shape,
            [place, rounds, slots, pair_irrep, orbital_irrep, orbital, *found, *held],
            [
                pltpu.VMEM((512, LANES), jnp.float32),
                pltpu.VMEM((16 * size, LANES), jnp.float32),
                pltpu.VMEM((2048, LANES), jnp.float32),
                pltpu.SemaphoreType.DMA((4,)),
            ],
            out_specs=jax.tree.map(lambda _: HBM, out_shape),
            any_last=len(held),
        )

    sent, slots, targets, mates, rounds, choice = plan(jnp.int32(0))
    near, v_high, v_low, sent, mates = lax.optimization_barrier((near, v_high, v_low, sent, mates))
    gathered = gather(sent, mates)

    def unpacked(filled):
        return filled.reshape(LANES, 4, 4, LANES).transpose(0, 2, 1, 3).reshape(LANES, 4, 512)

    def few(size, targets, gathered):
        found, _ = work(size, targets, gathered)
        return unpacked(spread(size, f32((2048, LANES)), rounds, slots, found))

    def many(targets, gathered):
        found, spare = work(SLOTS, targets, gathered)

        def later(state):
            turn, held = state
            sent, slots, targets, mates, _, _ = plan(turn)
            found, _ = work(SLOTS, targets, gather(sent, mates))
            return turn + 1, tuple(spread(SLOTS, [f32((1024, LANES))] * 2, rounds, slots, found, held))

        found, spare, turn = lax.optimization_barrier((found, spare, jnp.int32(1)))
        _, held = lax.while_loop(lambda state: state[0] < rounds[0], later, (turn, spare))
        return unpacked(spread(SLOTS, f32((2048, LANES)), rounds, slots, found, held))

    ways = [functools.partial(few, size) for size in FEWER] + [many]
    return lax.switch(choice[0], ways, targets, gathered)


def solution(mesh):
    devices = np.asarray(mesh.devices).reshape(4, 2, 16, 2, 2)
    fine = Mesh(devices, ("y", "xh", "z", "xl", "core"))
    blocks, groups = ("y", "xh", "z"), ("xl", "core")
    placed = (P(blocks, None, groups), P(None, groups, blocks, None), P(), P(), P())
    return jax.shard_map(
        on_device,
        mesh=fine,
        in_specs=placed,
        out_specs=P(groups, blocks, None),
        check_vma=False,
    )
```
